32 devices in a mesh: dp: 8 (over y, x, core), tensor: 4 (over z).
Axes of the slice: x: 2, y: 2, z: 4, core: 2. Of those that a mesh axis runs over, the one named last changes fastest.
Arguments:
- activations: bfloat16 [4608, 2560], P(('dp', 'tensor')), may hold values from -6 to 6
- out_grad: bfloat16 [4608, 6912], P('dp', 'tensor'), may hold values from -0.29882812 to 0.29882812
- error_state: bfloat16 [8, 6912, 2560], P('dp', 'tensor'), may hold values from -36 to 36
- right_factor: float32 [2560, 32], P('tensor'), may hold values from -6 to 6
Outputs:
- new_error: bfloat16 [8, 6912, 2560], P('dp', 'tensor')
- new_factor: float32 [2560, 32], P('tensor')
The draws below stay inside these ranges and needn't reach their ends.
All inputs are finite; a program needn't handle non-finite values.
Results may differ from the reference program's by a relative error of at most 0.0065.
Values may be sent and summed in bfloat16 or wider, within the bound.
No kernel may reach another device: no remote copies, remote signals or barrier semaphores. Data moves between devices by JAX's collectives and lax.ppermute only.
A program may use at most 128 MiB of HBM per device.

```python
import math
import jax
import jax.numpy as jnp
from jax import lax

D = 2560
FF = 6912
R = 32
TOK = 576
TOKENS = 4608
N_DP = 8


def draw_error_state(key, part):
    key = jax.random.fold_in(key, 11)
    keys = jax.random.split(key, 3)
    positions = jnp.arange(FF, dtype=jnp.float32) / max(FF - 1, 1)
    row_scale = (1.0 + 2.0 * positions) * jnp.exp(jax.random.uniform(keys[1], (FF,), jnp.float32) * math.log(10.0))
    col_scale = jnp.exp(jax.random.uniform(keys[2], (D,), jnp.float32) * math.log(10.0))
    noise = jax.random.truncated_normal(keys[0], -4.0, 4.0, (N_DP, FF, D), jnp.float32)
    values = 0.03 * noise * row_scale[None, :, None] * col_scale[None, None, :]
    return values.astype(jnp.bfloat16)


def block_scale(key, extent, cuts, smallest, largest):
    level, own = 1.0, jax.random.fold_in(key, 6)
    for dim, blocks in cuts:
        steps = jnp.exp(jax.random.uniform(jax.random.fold_in(own, dim), (blocks,), jnp.float32, smallest / len(cuts), largest / len(cuts)))
        level = level * jnp.repeat(steps, extent[dim] // blocks).reshape([-1 if axis == dim else 1 for axis in range(len(extent))])
    return level


def gaussian(key, dims, scale, bound, cuts=(), held_as=jnp.bfloat16):
    loudness = block_scale(key, dims, cuts, -0.22, 0.18) if cuts else 1.0
    result = jax.random.normal(key, dims, jnp.float32) * scale * loudness
    return jnp.minimum(jnp.maximum(result, -bound), bound).astype(held_as)


def setup_inputs(seed: int = 0) -> dict:
    key_of = jax.random.split(jax.random.key(seed), 5)
    return {
        "activations": gaussian(key_of[0], (TOKENS, D), 1.0, 6.0, ((0, 32),)),
        "out_grad": gaussian(key_of[1], (TOKENS, FF), 0.05, 0.29882812, ((0, 8), (1, 4))),
        "error_state": draw_error_state(jax.random.fold_in(key_of[4], 71), 0),
        "right_factor": gaussian(key_of[3], (D, R), 1.0, 6.0, ((0, 4),), jnp.float32),
    }


def reference(activations, out_grad, error_state, right_factor):
    highest = lax.Precision.HIGHEST
    token_rows = activations.reshape(N_DP, TOK, D)
    grad_rows = out_grad.reshape(N_DP, TOK, FF)
    contract_first = (((0,), (0,)), ((), ()))

    def left_term(running, items):
        x_rows, dy_rows, errors = items
        projected = jnp.dot(x_rows.astype(jnp.float32), right_factor, precision=highest)
        term = lax.dot_general(dy_rows.astype(jnp.float32), projected, contract_first, precision=highest)
        term = term + jnp.dot(errors.astype(jnp.float32), right_factor, precision=highest)
        return (running + term, None)
    p_total, _ = lax.scan(left_term, jnp.zeros((FF, R), jnp.float32), (token_rows, grad_rows, error_state))
    gram_matrix = jnp.dot(p_total.T, p_total, precision=highest)
    lower_factor = jnp.linalg.cholesky(gram_matrix)
    p_basis = lax.linalg.triangular_solve(lower_factor, p_total, left_side=False, lower=True, transpose_a=True)

    def right_term(running, items):
        x_rows, dy_rows, errors = items
        weighted = jnp.dot(dy_rows.astype(jnp.float32), p_basis, precision=highest)
        term = lax.dot_general(x_rows.astype(jnp.float32), weighted, contract_first, precision=highest)
        term = term + lax.dot_general(errors.astype(jnp.float32), p_basis, contract_first, precision=highest)
        return (running + term, None)
    summed, _ = lax.scan(right_term, jnp.zeros((D, R), jnp.float32), (token_rows, grad_rows, error_state))
    new_factor = summed / N_DP
    approx = jnp.dot(p_basis, new_factor.T, precision=highest)

    def rebuild(items):
        x_rows, dy_rows, errors = items
        grad = lax.dot_general(dy_rows.astype(jnp.float32), x_rows.astype(jnp.float32), contract_first, preferred_element_type=jnp.float32)
        corrected = grad + errors.astype(jnp.float32)
        return (corrected - approx).astype(jnp.bfloat16)
    new_error = lax.map(rebuild, (token_rows, grad_rows, error_state))
    return (new_error, new_factor)
```

```python
import functools
import jax
import jax.numpy as jnp
from jax import lax
from jax.experimental import pallas as pl
from jax.experimental.pallas import tpu as pltpu
from jax.sharding import PartitionSpec as P

contract_first = (((0,), (0,)), ((), ()))
contract_last = (((1,), (1,)), ((), ()))
column_block = 8
bf16, f32 = jnp.bfloat16, jnp.float32
MIB = 1 << 20


def plain_body(activations, out_grad, error_state, right_factor):
    highest = lax.Precision.HIGHEST
    errors = error_state[0]
    rows_here = right_factor.shape[0]
    factor_full = lax.all_gather(right_factor, "tensor", axis=0, tiled=True)
    grad = lax.dot_general(
        out_grad,
        lax.all_gather(activations, "tensor", axis=0, tiled=True),
        contract_first,
        preferred_element_type=f32,
    )
    corrected = grad + errors.astype(f32)
    p_local = jnp.dot(corrected, factor_full, precision=highest)
    p_total = lax.psum(p_local.astype(bf16), "dp").astype(f32)
    p_basis = jnp.zeros_like(p_total)
    for block_index in range(p_total.shape[1] // column_block):
        first = block_index * column_block
        columns = p_total[:, first : first + column_block]
        coeffs, block_gram = lax.psum(
            (
                jnp.dot(p_basis.T, columns, precision=highest),
                jnp.dot(columns.T, columns, precision=highest),
            ),
            "tensor",
        )
        remainder = columns - jnp.dot(p_basis, coeffs, precision=highest)
        residual_gram = block_gram - jnp.dot(coeffs.T, coeffs, precision=highest)
        lower_factor = jnp.linalg.cholesky(residual_gram)
        orthonormal = lax.linalg.triangular_solve(
            lower_factor, remainder, left_side=False, lower=True, transpose_a=True
        )
        p_basis = p_basis.at[:, first : first + column_block].set(orthonormal)
    replicas = lax.axis_size("dp")
    term = lax.dot_general(corrected, p_basis, contract_first, precision=highest)
    summed = lax.psum(term, ("dp", "tensor")) / replicas
    new_error = (corrected - jnp.dot(p_basis, summed.T, precision=highest)).astype(bf16)
    new_factor = lax.dynamic_slice_in_dim(
        summed, lax.axis_index("tensor") * rows_here, rows_here, 0
    )
    return (new_error[None], new_factor)


def dot(a, b, dims=None, precision=None):
    if dims is None:
        dims = (((1,), (0,)), ((), ()))
    return lax.dot_general(a, b, dims, precision=precision, preferred_element_type=f32)


def split(v):
    high = v.astype(bf16)
    return high, (v - high.astype(f32)).astype(bf16)


def call(kernel, outs, *args, scratch=(), grid=None, in_specs=None, out_specs=None, vmem=48, flops=0, moved=0):
    vmem_spec = pl.BlockSpec(memory_space=pltpu.VMEM)
    if grid is None:
        in_specs = [
            pl.BlockSpec(memory_space=pltpu.SMEM) if a.dtype == jnp.int32 else vmem_spec
            for a in args
        ]
        out_specs = [vmem_spec] * len(outs)
        extra = {}
    else:
        extra = {"grid": grid}
    size = sum(a.size * a.dtype.itemsize for a in args) + sum(
        o.size * o.dtype.itemsize for o in outs
    )
    result = pl.pallas_call(
        kernel,
        out_shape=list(outs),
        in_specs=in_specs,
        out_specs=out_specs,
        scratch_shapes=list(scratch),
        compiler_params=pltpu.CompilerParams(vmem_limit_bytes=vmem * MIB),
        cost_estimate=pl.CostEstimate(flops=flops, bytes_accessed=size, transcendentals=0),
        name=kernel.__name__ if hasattr(kernel, "__name__") else kernel.func.__name__,
        **extra,
    )(*args)
    return result


def like(shape, dtype):
    return jax.ShapeDtypeStruct(shape, dtype)


def flip_factor(q_ref, out_ref):
    out_ref[...] = q_ref[...].T.astype(bf16)


def project(place, own, n1, n2, n3, x_ref, q_ref, y_ref):
    t = place[0]
    for k, part in enumerate((own, n1, n2, n3)):
        q_ref[t ^ k] = part[...]
    parts, _, width = q_ref.shape
    total = dot(q_ref[0], x_ref[:, :width], contract_last)
    for k in range(1, parts):
        total += dot(q_ref[k], x_ref[:, k * width : (k + 1) * width], contract_last)
    y_ref[...] = total


def error_left(q_ref, e_ref, out_ref):
    term = dot(q_ref[0], e_ref[...], contract_last)

    @pl.when(pl.program_id(0) == 0)
    def _():
        out_ref[...] = term

    @pl.when(pl.program_id(0) > 0)
    def _():
        out_ref[...] += term


def left_factor(place, eq_ref, own, n1, n2, n3, dy_ref, out_ref, y4):
    t = place[0]
    for k, part in enumerate((own, n1, n2, n3)):
        y4[t ^ k] = part[...]
    parts, rank, tokens = y4.shape
    total = eq_ref[...]
    for s in range(parts):
        both = jnp.concatenate(split(y4[s]), axis=0)
        term = dot(both, dy_ref[s * tokens : (s + 1) * tokens, :])
        total += term[:rank] + term[rank:]
    out_ref[...] = total.astype(bf16)


def weigh(place, own, n1, n2, n3, dy_ref, p_ref, m0, m1, m2, m3, held):
    t = place[0]
    p = (own[...].astype(f32) + n1[...].astype(f32)) + (n2[...].astype(f32) + n3[...].astype(f32))
    p = p.astype(bf16)
    p_ref[...] = p
    parts, rank, tokens = held.shape
    gram = dot(p, p, contract_last)
    for s in range(parts):
        held[s] = dot(p, dy_ref[s * tokens : (s + 1) * tokens, :], contract_last)
    for k, out in enumerate((m0, m1, m2, m3)):
        out[:, :tokens] = held[t ^ k]
        out[:, 256 : 256 + rank] = gram


def error_right(p_ref, e_ref, out_ref):
    out_ref[...] = dot(p_ref[...], e_ref[...])


def right_term(place, m0, m1, m2, m3, te_ref, x_ref, gram_ref, keep_ref, send_ref, held):
    core = place[1]
    tokens = x_ref.shape[0]
    rank = te_ref.shape[0]
    total = (m0[...] + m1[...]) + (m2[...] + m3[...])
    gram_ref[...] = total[:, 256 : 256 + rank]
    both = jnp.concatenate(split(total[:, :tokens]), axis=0)
    term = dot(both, x_ref[...])
    term = te_ref[...] + (term[:rank] + term[rank:])
    held[0] = term[: rank // 2]
    held[1] = term[rank // 2 :]
    keep_ref[...] = held[core]
    send_ref[...] = held[1 - core]


def cut(place, keep, got, o0, o1, o2, o3, held):
    t = place[0]
    total = keep[...] + got[...]
    width = held.shape[2]
    for s in range(held.shape[0]):
        held[s] = total[:, s * width : (s + 1) * width]
    for k, out in enumerate((o0, o1, o2, o3)):
        out[...] = held[t ^ k]


def invert_cholesky(g_ref, out_ref):
    n = g_ref.shape[0]
    rows = lax.broadcasted_iota(jnp.int32, (n, n), 0)
    cols = lax.broadcasted_iota(jnp.int32, (n, n), 1)
    a = g_ref[...]
    inverse = jnp.where(rows == cols, 1.0, 0.0).astype(f32)
    for j in range(n):
        column = jnp.sum(jnp.where(cols == j, a, 0.0), axis=1, keepdims=True)
        pivot = column[j : j + 1, :]
        factor = jnp.where(rows[:, :1] > j, column / pivot, 0.0)
        a = a - factor * a[j : j + 1, :]
        inverse = inverse - factor * inverse[j : j + 1, :]
    diagonal = jnp.sum(jnp.where(rows == cols, a, 0.0), axis=1, keepdims=True)
    out_ref[...] = inverse * lax.rsqrt(diagonal)


def flip_grad(dy_ref, main_ref, rest_ref):
    main = main_ref.shape[1]
    main_ref[...] = dy_ref[:main, :].T
    rest_ref[...] = dy_ref[main:, :].T


def finish_factor(replicas, place, linv, p_ref, rest_ref, a0, a1, a2, a3, b0, b1, b2, b3, left_ref, right_ref, new_ref, held, nf4):
    t, core = place[0], place[1]
    for k, (a, b) in enumerate(((a0, b0), (a1, b1), (a2, b2), (a3, b3))):
        held[t ^ k, core] = a[...]
        held[t ^ k, 1 - core] = b[...]
    highest = lax.Precision.HIGHEST
    parts, _, half, width = held.shape
    rank = 2 * half
    scaled = linv[...] * (1.0 / replicas)
    for s in range(parts):
        nf = dot(scaled, held[s].reshape(rank, width), precision=highest)
        nf4[s] = nf
        high, low = split(nf)
        at = slice(s * width, (s + 1) * width)
        right_ref[:rank, at] = high
        right_ref[rank : 2 * rank, at] = high
        right_ref[2 * rank :, at] = low
    new_ref[...] = nf4[t].T
    basis = dot(linv[...], p_ref[...].astype(f32), precision=highest)
    high, low = split(-basis)
    rest = rest_ref.shape[1]
    left_ref[:, :rest] = rest_ref[...]
    left_ref[:, rest:] = jnp.concatenate((high, low, high), axis=0).T


def rebuild(main_ref, left_ref, x_ref, right_ref, e_ref, out_ref, tail):
    main = main_ref.shape[1]
    rest = x_ref.shape[0] - main

    @pl.when(pl.program_id(0) == 0)
    def _():
        tail[:rest, :] = x_ref[main:, :]
        tail[rest:, :] = right_ref[...]

    step = 512
    for c in range(0, x_ref.shape[1], step):
        at = slice(c, c + step)
        total = dot(main_ref[...], x_ref[:main, at]) + dot(left_ref[...], tail[:, at])
        out_ref[:, at] = (total + e_ref[:, at].astype(f32)).astype(bf16)


def partners(value, axis, size, by):
    return [lax.ppermute(value, axis, [(i, i ^ k) for i in range(size)]) for k in by]


def body(activations, out_grad, error_state, right_factor):
    errors = error_state[0]
    n_dp, n_t = lax.axis_size("dp"), lax.axis_size("tensor")
    rows, rank = right_factor.shape
    tokens, features = activations.shape
    all_tokens, hidden = out_grad.shape
    place = jnp.stack([lax.axis_index("tensor"), lax.axis_index("dp") % 2]).astype(jnp.int32)
    along_t = functools.partial(partners, axis="tensor", size=n_t, by=(1, 2, 3))
    along_xy = functools.partial(partners, axis="dp", size=n_dp, by=(2, 4, 6))

    x_full = lax.all_gather(activations, "tensor", axis=0, tiled=True)

    (q_own,) = call(flip_factor, [like((rank, rows), bf16)], right_factor)
    q_parts = along_t(q_own)
    main = all_tokens // 256 * 256
    main_t, rest_t = call(
        flip_grad,
        [like((hidden, main), bf16), like((hidden, all_tokens - main), bf16)],
        out_grad,
    )
    q_full, y_own = call(
        project,
        [like((n_t, rank, rows), bf16), like((rank, tokens), f32)],
        place, q_own, *q_parts, activations,
    )
    y_parts = along_t(y_own)
    (eq,) = call(
        error_left,
        [like((rank, hidden), f32)],
        q_full, errors,
        grid=(n_t,),
        in_specs=[
            pl.BlockSpec((1, rank, rows), lambda k: (k, 0, 0)),
            pl.BlockSpec((hidden, rows), lambda k: (0, k)),
        ],
        out_specs=[pl.BlockSpec((rank, hidden), lambda k: (0, 0))],
    )
    (p_local,) = call(
        left_factor,
        [like((rank, hidden), bf16)],
        place, eq, y_own, *y_parts, out_grad,
        scratch=[pltpu.VMEM((n_t, rank, tokens), f32)],
    )
    (p_other,) = partners(p_local, "dp", n_dp, (1,))
    p_chip = (p_local.astype(f32) + p_other.astype(f32)).astype(bf16)
    p_parts = along_xy(p_chip)
    p_total, *messages = call(
        weigh,
        [like((rank, hidden), bf16)] + [like((rank, 384), f32)] * 4,
        place, p_chip, *p_parts, out_grad,
        scratch=[pltpu.VMEM((n_t, rank, tokens), f32)],
    )
    arrived = [
        lax.ppermute(m, "tensor", [(i, i ^ k) for i in range(n_t)])
        for k, m in enumerate(messages)
        if k
    ]
    (te,) = call(
        error_right,
        [like((rank, features), f32)],
        p_total, errors,
        grid=(n_t,),
        in_specs=[
            pl.BlockSpec((rank, hidden), lambda k: (0, 0)),
            pl.BlockSpec((hidden, rows), lambda k: (0, k)),
        ],
        out_specs=[pl.BlockSpec((rank, rows), lambda k: (0, k))],
    )
    gram, keep, send = call(
        right_term,
        [like((rank, rank), f32), like((rank // 2, features), f32), like((rank // 2, features), f32)],
        place, messages[0], *arrived, te, activations,
        scratch=[pltpu.VMEM((2, rank // 2, features), f32)],
    )
    (got,) = partners(send, "dp", n_dp, (1,))
    (linv,) = call(invert_cholesky, [like((rank, rank), f32)], gram)
    pieces = call(
        cut,
        [like((rank // 2, rows), f32)] * 4,
        place, keep, got,
        scratch=[pltpu.VMEM((n_t, rank // 2, rows), f32)],
    )
    arrived = [
        lax.ppermute(m, "tensor", [(i, i ^ k) for i in range(n_t)])
        for k, m in enumerate(pieces)
        if k
    ]
    mine = (pieces[0] + arrived[0]) + (arrived[1] + arrived[2])
    x_side, y_side, diagonal = along_xy(mine)
    mine = (mine + x_side) + (y_side + diagonal)
    near = [mine] + along_t(mine)
    far = [partners(v, "dp", n_dp, (1,))[0] for v in near]
    left, right, new_factor = call(
        functools.partial(finish_factor, n_dp),
        [like((hidden, all_tokens - main + 3 * rank), bf16), like((3 * rank, features), bf16), like((rows, rank), f32)],
        place, linv, p_total, rest_t, *near, *far,
        scratch=[pltpu.VMEM((n_t, 2, rank // 2, rows), f32), pltpu.VMEM((n_t, rank, rows), f32)],
    )
    steps = 6
    block = hidden // steps
    (new_error,) = call(
        rebuild,
        [like((hidden, features), bf16)],
        main_t, left, x_full, right, errors,
        grid=(steps,),
        in_specs=[
            pl.BlockSpec((block, main), lambda k: (k, 0)),
            pl.BlockSpec((block, left.shape[1]), lambda k: (k, 0)),
            pl.BlockSpec((all_tokens, features), lambda k: (0, 0)),
            pl.BlockSpec((3 * rank, features), lambda k: (0, 0)),
            pl.BlockSpec((block, features), lambda k: (k, 0)),
        ],
        out_specs=[pl.BlockSpec((block, features), lambda k: (k, 0))],
        scratch=[pltpu.VMEM((left.shape[1], features), bf16)],
    )
    return (new_error[None], new_factor)


def solution(mesh):
    placed = (
        P(("dp", "tensor"), None),
        P("dp", "tensor"),
        P("dp", "tensor", None),
        P("tensor", None),
    )
    fits = mesh.shape["dp"] == 8 and mesh.shape["tensor"] == 4
    return jax.shard_map(
        body if fits else plain_body,
        mesh=mesh,
        in_specs=placed,
        out_specs=(P("dp", "tensor", None), P("tensor", None)),
        check_vma=False,
    )
```

```python
import functools
import jax
import jax.numpy as jnp
from jax import lax
from jax.experimental import pallas as pl
from jax.experimental.pallas import tpu as pltpu
from jax.sharding import PartitionSpec as P

contract_first = (((0,), (0,)), ((), ()))
contract_last = (((1,), (1,)), ((), ()))
column_block = 8
bf16, f32 = jnp.bfloat16, jnp.float32
MIB = 1 << 20


def plain_body(activations, out_grad, error_state, right_factor):
    highest = lax.Precision.HIGHEST
    errors = error_state[0]
    rows_here = right_factor.shape[0]
    factor_full = lax.all_gather(right_factor, "tensor", axis=0, tiled=True)
    grad = lax.dot_general(
        out_grad,
        lax.all_gather(activations, "tensor", axis=0, tiled=True),
        contract_first,
        preferred_element_type=f32,
    )
    corrected = grad + errors.astype(f32)
    p_local = jnp.dot(corrected, factor_full, precision=highest)
    p_total = lax.psum(p_local.astype(bf16), "dp").astype(f32)
    p_basis = jnp.zeros_like(p_total)
    for block_index in range(p_total.shape[1] // column_block):
        first = block_index * column_block
        columns = p_total[:, first : first + column_block]
        coeffs, block_gram = lax.psum(
            (
                jnp.dot(p_basis.T, columns, precision=highest),
                jnp.dot(columns.T, columns, precision=highest),
            ),
            "tensor",
        )
        remainder = columns - jnp.dot(p_basis, coeffs, precision=highest)
        residual_gram = block_gram - jnp.dot(coeffs.T, coeffs, precision=highest)
        lower_factor = jnp.linalg.cholesky(residual_gram)
        orthonormal = lax.linalg.triangular_solve(
            lower_factor, remainder, left_side=False, lower=True, transpose_a=True
        )
        p_basis = p_basis.at[:, first : first + column_block].set(orthonormal)
    replicas = lax.axis_size("dp")
    term = lax.dot_general(corrected, p_basis, contract_first, precision=highest)
    summed = lax.psum(term, ("dp", "tensor")) / replicas
    new_error = (corrected - jnp.dot(p_basis, summed.T, precision=highest)).astype(bf16)
    new_factor = lax.dynamic_slice_in_dim(
        summed, lax.axis_index("tensor") * rows_here, rows_here, 0
    )
    return (new_error[None], new_factor)


def dot(a, b, dims=None, precision=None):
    if dims is None:
        dims = (((1,), (0,)), ((), ()))
    return lax.dot_general(a, b, dims, precision=precision, preferred_element_type=f32)


def split(v):
    high = v.astype(bf16)
    return high, (v - high.astype(f32)).astype(bf16)


def call(kernel, outs, *args, scratch=(), grid=None, in_specs=None, out_specs=None, vmem=8, flops=0, moved=0):
    vmem_spec = pl.BlockSpec(memory_space=pltpu.VMEM)
    if in_specs is None:
        in_specs = [
            pl.BlockSpec(memory_space=pltpu.SMEM) if a.dtype == jnp.int32 else vmem_spec
            for a in args
        ]
    if out_specs is None:
        out_specs = [vmem_spec] * len(outs)
    extra = {} if grid is None else {"grid": grid}
    size = sum(a.size * a.dtype.itemsize for a in args) + sum(
        o.size * o.dtype.itemsize for o in outs
    )
    result = pl.pallas_call(
        kernel,
        out_shape=list(outs),
        in_specs=in_specs,
        out_specs=out_specs,
        scratch_shapes=list(scratch),
        compiler_params=pltpu.CompilerParams(vmem_limit_bytes=vmem * MIB),
        cost_estimate=pl.CostEstimate(flops=flops, bytes_accessed=size, transcendentals=0),
        **extra,
        name=kernel.__name__ if hasattr(kernel, "__name__") else kernel.func.__name__,
    )(*args)
    return result


def like(shape, dtype):
    return jax.ShapeDtypeStruct(shape, dtype)


def project(place, own, n1, n2, n3, x_ref, q_ref, y_ref):
    t = place[0]
    for k, part in enumerate((own, n1, n2, n3)):
        q_ref[t ^ k] = part[...]
    parts, _, width = q_ref.shape
    total = dot(q_ref[0], x_ref[:, :width], contract_last)
    for k in range(1, parts):
        total += dot(q_ref[k], x_ref[:, k * width : (k + 1) * width], contract_last)
    y_ref[...] = total


def error_left(q_ref, e_ref, out_ref):
    term = dot(q_ref[0], e_ref[...], contract_last)

    @pl.when(pl.program_id(0) == 0)
    def _():
        out_ref[...] = term

    @pl.when(pl.program_id(0) > 0)
    def _():
        out_ref[...] += term


def left_factor(place, eq_ref, own, n1, n2, n3, dy_ref, out_ref, y4):
    t = place[0]
    for k, part in enumerate((own, n1, n2, n3)):
        y4[t ^ k] = part[...]
    parts, rank, tokens = y4.shape
    total = eq_ref[...]
    for s in range(parts):
        both = jnp.concatenate(split(y4[s]), axis=0)
        term = dot(both, dy_ref[s * tokens : (s + 1) * tokens, :])
        total += term[:rank] + term[rank:]
    out_ref[...] = total.astype(bf16)


def first_partner(t):
    return jnp.where((t == 1) | (t == 2), 2, 1)


def weigh(place, own, n1, n2, n3, dy_ref, p_ref, gram_ref, near_ref, far_ref, held):
    t = place[0]
    p = (own[...].astype(f32) + n1[...].astype(f32)) + (n2[...].astype(f32) + n3[...].astype(f32))
    p = p.astype(bf16)
    p_ref[...] = p
    parts, _, tokens = held.shape
    gram_ref[...] = dot(p, p, contract_last)
    for s in range(parts):
        held[s] = dot(p, dy_ref[s * tokens : (s + 1) * tokens, :], contract_last)
    step = first_partner(t)
    near_ref[0] = held[t]
    near_ref[1] = held[t ^ step]
    far_ref[0] = held[t ^ 3]
    far_ref[1] = held[t ^ 3 ^ step]


def error_right(p_ref, e_ref, out_ref):
    out_ref[...] = dot(p_ref[...], e_ref[...])


def right_term(place, near_ref, got_ref, te_ref, x_own, x_first, keep_ref, send_ref, held):
    core = place[1]
    rank = te_ref.shape[0]
    total = te_ref[...]
    for k, x_ref in enumerate((x_own, x_first)):
        both = jnp.concatenate(split(near_ref[k] + got_ref[k]), axis=0)
        term = dot(both, x_ref[...])
        total += term[:rank] + term[rank:]
    held[0] = total[: rank // 2]
    held[1] = total[rank // 2 :]
    keep_ref[...] = held[core]
    send_ref[...] = held[1 - core]


def cut(place, keep, got, o0, o1, o2, o3, held):
    chip = place[2]
    total = keep[...] + got[...]
    width = held.shape[2]
    for s in range(held.shape[0]):
        held[s] = total[:, s * width : (s + 1) * width]
    for k, out in enumerate((o0, o1, o2, o3)):
        out[...] = held[chip ^ k]


def pack(a, b, c, d, gram_ref, out_ref):
    half, width = a.shape
    rank = 2 * half
    out_ref[...] = jnp.zeros_like(out_ref)
    out_ref[:, :width] = (a[...] + b[...]) + (c[...] + d[...])
    out_ref[:, width : width + rank] = gram_ref[:half, :]
    out_ref[:, width + 128 : width + 128 + rank] = gram_ref[half:, :]


def unpack(a, b, c, d, out_ref, gram_ref):
    half, width = out_ref.shape
    rank = 2 * half
    total = (a[...] + b[...]) + (c[...] + d[...])
    out_ref[...] = total[:, :width]
    gram_ref[:half, :] = total[:, width : width + rank]
    gram_ref[half:, :] = total[:, width + 128 : width + 128 + rank]


def invert_cholesky(g_ref, out_ref):
    n = g_ref.shape[0]
    rows = lax.broadcasted_iota(jnp.int32, (n, n), 0)
    cols = lax.broadcasted_iota(jnp.int32, (n, n), 1)
    a = g_ref[...]
    inverse = jnp.where(rows == cols, 1.0, 0.0).astype(f32)
    for j in range(n):
        column = jnp.sum(jnp.where(cols == j, a, 0.0), axis=1, keepdims=True)
        pivot = column[j : j + 1, :]
        factor = jnp.where(rows[:, :1] > j, column / pivot, 0.0)
        a = a - factor * a[j : j + 1, :]
        inverse = inverse - factor * inverse[j : j + 1, :]
    diagonal = jnp.sum(jnp.where(rows == cols, a, 0.0), axis=1, keepdims=True)
    out_ref[...] = inverse * lax.rsqrt(diagonal)


def arrange(place, dy_any, dy_ref, main_ref, rest_ref, held, sem):
    copy = pltpu.make_async_copy(dy_any, dy_ref, sem)
    copy.start()
    t = place[0]
    step = first_partner(t)
    tokens = rest_ref.shape[1]
    copy.wait()
    for k, source in enumerate((t, t ^ step, t ^ 3 ^ step, t ^ 3)):
        held[k * tokens : (k + 1) * tokens, :] = dy_ref[pl.ds(pl.multiple_of(source * tokens, tokens), tokens), :]
    main = main_ref.shape[1]
    main_ref[...] = held[:main, :].T
    rest_ref[...] = held[main:, :].T


def accumulate(first, main_ref, e_any, x_own, x_first, x_second, acc_ref, x_ref, e_ref, e_sem, sems):
    width = acc_ref.shape[1]
    tokens = x_own.shape[0]
    copies = [pltpu.make_async_copy(e_any.at[:, pl.ds(first, width)], e_ref, e_sem)]
    for k, source in enumerate((x_own, x_first, x_second)):
        copies.append(
            pltpu.make_async_copy(source.at[:, pl.ds(first, width)], x_ref.at[pl.ds(k * tokens, tokens), :], sems.at[k])
        )
    for copy in copies:
        copy.start()
    for copy in copies:
        copy.wait()
    step, block = 640, 432
    for c in range(0, width, step):
        cols = slice(c, c + step)
        for r in range(0, acc_ref.shape[0], block):
            at = slice(r, r + block)
            acc_ref[at, cols] = dot(main_ref[at, :], x_ref[:, cols]) + e_ref[at, cols].astype(f32)


def rebuild(replicas, place, linv, p_ref, rest_ref, a0, a1, a2, a3, b0, b1, b2, b3, acc_0, acc_1, outer, inner,
            new_ref, out_any, held, nf4, left_ref, buffer, staged, sems, out_sems):
    rows = inner.shape[0]
    t, core, chip = place[0], place[1], place[2]
    is_inner = (t == 1) | (t == 2)

    def fetch(source):
        return pltpu.make_async_copy(source, buffer.at[pl.ds(0, rows), :], sems.at[0])

    @pl.when(is_inner)
    def _():
        fetch(inner).start()

    @pl.when(jnp.logical_not(is_inner))
    def _():
        fetch(outer).start()

    for k, (a, b) in enumerate(((a0, b0), (a1, b1), (a2, b2), (a3, b3))):
        held[chip ^ k, core] = a[...]
        held[chip ^ k, 1 - core] = b[...]
    highest = lax.Precision.HIGHEST
    parts, _, half, width = held.shape
    rank = 2 * half
    base = rows
    scaled = linv[...] * (1.0 / replicas)
    for s in range(parts):
        nf = dot(scaled, held[s].reshape(rank, width), precision=highest)
        nf4[s] = nf
        high, low = split(nf)
        at = slice(s * width, (s + 1) * width)
        buffer[base : base + rank, at] = high
        buffer[base + rank : base + 2 * rank, at] = high
        buffer[base + 2 * rank :, at] = low
    new_ref[...] = nf4[t]
    basis = dot(linv[...], p_ref[...].astype(f32), precision=highest)
    high, low = split(-basis)
    left_ref[:, :base] = rest_ref[...]
    left_ref[:, base:] = jnp.concatenate((high, low, high), axis=0).T
    fetch(inner).wait()
    width = staged.shape[2]
    count = acc_0.shape[1] // width

    def put(i, slot):
        return pltpu.make_async_copy(staged.at[slot], out_any.at[:, pl.ds(pl.multiple_of(i * width, width), width)], out_sems.at[slot])

    for part, acc_ref in enumerate((acc_0, acc_1)):

        @pl.loop(0, count)
        def _(c):
            i = part * count + c
            slot = lax.rem(i, 2)

            @pl.when(i >= 2)
            def _():
                put(i - 2, slot).wait()

            here = pl.ds(pl.multiple_of(c * width, width), width)
            cols = pl.ds(pl.multiple_of(i * width, width), width)
            block = 432
            for r in range(0, acc_ref.shape[0], block):
                at = slice(r, r + block)
                total = acc_ref[at, here] + dot(left_ref[at, :], buffer[:, cols])
                staged[slot, at, :] = total.astype(bf16)
            put(i, slot).start()

    for i in (2 * count - 2, 2 * count - 1):
        put(i, i % 2).wait()


def after(value, *others):
    return lax.optimization_barrier((value, *others))[0]


def partners(value, axis, size, by):
    return [lax.ppermute(value, axis, [(i, i ^ k) for i in range(size)]) for k in by]


def body(activations, out_grad, error_state, right_factor):
    errors = error_state[0]
    n_dp, n_t = lax.axis_size("dp"), lax.axis_size("tensor")
    rows, rank = right_factor.shape
    tokens, features = activations.shape
    all_tokens, hidden = out_grad.shape
    half = rank // 2
    t, d = lax.axis_index("tensor"), lax.axis_index("dp")
    place = jnp.stack([t, d & 1, d >> 1]).astype(jnp.int32)
    along_t = functools.partial(partners, axis="tensor", size=n_t, by=(1, 2, 3))
    along_xy = functools.partial(partners, axis="dp", size=n_dp, by=(2, 4, 6))

    anywhere = pl.BlockSpec(memory_space=pl.ANY)
    vmem_spec = pl.BlockSpec(memory_space=pltpu.VMEM)
    smem_spec = pl.BlockSpec(memory_space=pltpu.SMEM)
    hbm_spec = pl.BlockSpec(memory_space=pltpu.HBM)

    def move(value, perm, *when):
        return lax.ppermute(after(value, *when), "tensor", perm)

    q_own = right_factor.T.astype(bf16)
    q_parts = along_t(q_own)

    main = 3 * tokens
    grads, main_t, rest_t = call(
        arrange,
        [like((all_tokens, hidden), bf16), like((hidden, main), bf16), like((hidden, tokens), bf16)],
        place, out_grad,
        in_specs=[smem_spec, hbm_spec],
        scratch=[pltpu.VMEM((all_tokens, hidden), bf16), pltpu.SemaphoreType.DMA(())],
        vmem=50,
    )
    q_parts, _ = lax.optimization_barrier((q_parts, main_t))
    q_full, y_own = call(
        project,
        [like((n_t, rank, rows), bf16), like((rank, tokens), f32)],
        place, q_own, *q_parts, activations,
    )
    y_parts = along_t(y_own)
    (eq,) = call(
        error_left,
        [like((rank, hidden), f32)],
        q_full, errors,
        grid=(n_t,),
        in_specs=[
            pl.BlockSpec((1, rank, rows), lambda k: (k, 0, 0)),
            pl.BlockSpec((hidden, rows), lambda k: (0, k)),
        ],
        out_specs=[pl.BlockSpec((rank, hidden), lambda k: (0, 0))],
        vmem=50,
    )
    y_parts[0] = after(y_parts[0], eq)
    x_first = move(activations, [(0, 2), (2, 3), (3, 1), (1, 0)], *y_parts)
    (p_local,) = call(
        left_factor,
        [like((rank, hidden), bf16)],
        place, eq, y_own, *y_parts, grads,
        scratch=[pltpu.VMEM((n_t, rank, tokens), f32)],
    )
    (p_other,) = partners(p_local, "dp", n_dp, (1,))
    p_chip = (p_local.astype(f32) + p_other.astype(f32)).astype(bf16)
    p_parts = along_xy(p_chip)
    p_parts[0] = after(p_parts[0], x_first)
    p_total, gram, near_w, far_w = call(
        weigh,
        [like((rank, hidden), bf16), like((rank, rank), f32), like((2, rank, tokens), f32), like((2, rank, tokens), f32)],
        place, p_chip, *p_parts, grads,
        scratch=[pltpu.VMEM((n_t, rank, tokens), f32)],
    )
    (got_w,) = partners(far_w, "tensor", n_t, (3,))
    (te,) = call(
        error_right,
        [like((rank, features), f32)],
        p_total, errors,
        grid=(n_t,),
        in_specs=[
            pl.BlockSpec((rank, hidden), lambda k: (0, 0)),
            pl.BlockSpec((hidden, rows), lambda k: (0, k)),
        ],
        out_specs=[pl.BlockSpec((rank, rows), lambda k: (0, k))],
        vmem=50,
    )
    got_w = after(got_w, te)
    keep, given = call(
        right_term,
        [like((half, features), f32), like((half, features), f32)],
        place, near_w, got_w, te, activations, x_first,
        scratch=[pltpu.VMEM((2, half, features), f32)],
    )
    x_second = move(activations, [(0, 1), (1, 3), (3, 2), (2, 0)], got_w)
    (got,) = partners(given, "dp", n_dp, (1,))
    parts = call(
        cut,
        [like((half, rows), f32)] * 4,
        place, keep, got,
        scratch=[pltpu.VMEM((n_t, half, rows), f32)],
    )
    arrived = [
        lax.ppermute(m, "dp", [(i, i ^ (2 * k)) for i in range(n_dp)])
        for k, m in enumerate(parts)
        if k
    ]
    accs = []
    for first in (0, features // 2):
        accs += call(
            functools.partial(accumulate, first),
            [like((hidden, features // 2), f32)],
            main_t, errors, activations, x_first, x_second,
            in_specs=[vmem_spec, hbm_spec] + [anywhere] * 3,
            scratch=[
                pltpu.VMEM((main, features // 2), bf16),
                pltpu.VMEM((hidden, features // 2), bf16),
                pltpu.SemaphoreType.DMA(()),
                pltpu.SemaphoreType.DMA((3,)),
            ],
            vmem=12,
        )
    (mine,) = call(pack, [like((half, rows + 256), f32)], parts[0], *arrived, gram)
    mine = after(mine, x_second)
    z1, z2, z3 = along_t(mine)
    to_outer_3 = move(x_first, [(1, 0), (2, 3)], z1, z2, z3)
    to_inner_3 = move(activations, [(1, 2), (2, 1)], z1, z2, z3)
    mine, gram = call(unpack, [like((half, rows), f32), like((rank, rank), f32)], mine, z1, z2, z3)
    (linv,) = call(invert_cholesky, [like((rank, rank), f32)], gram)
    near = [mine] + along_xy(mine)
    near[1] = after(near[1], linv)
    far = [partners(v, "dp", n_dp, (1,))[0] for v in near]
    new_factor, new_error = call(
        functools.partial(rebuild, n_dp),
        [like((rank, rows), f32), like((hidden, features), bf16)],
        place, linv, p_total, rest_t, *near, *far, *accs, to_outer_3, to_inner_3,
        in_specs=[smem_spec] + [vmem_spec] * 13 + [anywhere] * 2,
        out_specs=[vmem_spec, anywhere],
        scratch=[
            pltpu.VMEM((4, 2, half, rows), f32),
            pltpu.VMEM((n_t, rank, rows), f32),
            pltpu.VMEM((hidden, tokens + 3 * rank), bf16),
            pltpu.VMEM((tokens + 3 * rank, features), bf16),
            pltpu.VMEM((2, hidden, 640), bf16),
            pltpu.SemaphoreType.DMA((1,)),
            pltpu.SemaphoreType.DMA((2,)),
        ],
    )
    return (new_error[None], new_factor.T)


def solution(mesh):
    placed = (
        P(("dp", "tensor"), None),
        P("dp", "tensor"),
        P("dp", "tensor", None),
        P("tensor", None),
    )
    fits = mesh.shape["dp"] == 8 and mesh.shape["tensor"] == 4
    return jax.shard_map(
        body if fits else plain_body,
        mesh=mesh,
        in_specs=placed,
        out_specs=(P("dp", "tensor", None), P("tensor", None)),
        check_vma=False,
    )
```

```python
import functools
import jax
import jax.numpy as jnp
from jax import lax
from jax.experimental import pallas as pl
from jax.experimental.pallas import tpu as pltpu
from jax.sharding import PartitionSpec as P

contract_first = (((0,), (0,)), ((), ()))
contract_last = (((1,), (1,)), ((), ()))
column_block = 8
bf16, f32 = jnp.bfloat16, jnp.float32
MIB = 1 << 20
KA, KB, KP = 1_000_000_000, 5_500_000_000, 3_500_000_000


def plain_body(activations, out_grad, error_state, right_factor):
    highest = lax.Precision.HIGHEST
    errors = error_state[0]
    rows_here = right_factor.shape[0]
    factor_full = lax.all_gather(right_factor, "tensor", axis=0, tiled=True)
    grad = lax.dot_general(
        out_grad,
        lax.all_gather(activations, "tensor", axis=0, tiled=True),
        contract_first,
        preferred_element_type=f32,
    )
    corrected = grad + errors.astype(f32)
    p_local = jnp.dot(corrected, factor_full, precision=highest)
    p_total = lax.psum(p_local.astype(bf16), "dp").astype(f32)
    p_basis = jnp.zeros_like(p_total)
    for block_index in range(p_total.shape[1] // column_block):
        first = block_index * column_block
        columns = p_total[:, first : first + column_block]
        coeffs, block_gram = lax.psum(
            (
                jnp.dot(p_basis.T, columns, precision=highest),
                jnp.dot(columns.T, columns, precision=highest),
            ),
            "tensor",
        )
        remainder = columns - jnp.dot(p_basis, coeffs, precision=highest)
        residual_gram = block_gram - jnp.dot(coeffs.T, coeffs, precision=highest)
        lower_factor = jnp.linalg.cholesky(residual_gram)
        orthonormal = lax.linalg.triangular_solve(
            lower_factor, remainder, left_side=False, lower=True, transpose_a=True
        )
        p_basis = p_basis.at[:, first : first + column_block].set(orthonormal)
    replicas = lax.axis_size("dp")
    term = lax.dot_general(corrected, p_basis, contract_first, precision=highest)
    summed = lax.psum(term, ("dp", "tensor")) / replicas
    new_error = (corrected - jnp.dot(p_basis, summed.T, precision=highest)).astype(bf16)
    new_factor = lax.dynamic_slice_in_dim(
        summed, lax.axis_index("tensor") * rows_here, rows_here, 0
    )
    return (new_error[None], new_factor)


def dot(a, b, dims=None, precision=None):
    if dims is None:
        dims = (((1,), (0,)), ((), ()))
    return lax.dot_general(a, b, dims, precision=precision, preferred_element_type=f32)


def split(v):
    high = v.astype(bf16)
    return high, (v - high.astype(f32)).astype(bf16)


def call(kernel, outs, *args, scratch=(), grid=None, in_specs=None, out_specs=None, vmem=8, flops=0, moved=0):
    vmem_spec = pl.BlockSpec(memory_space=pltpu.VMEM)
    if in_specs is None:
        in_specs = [
            pl.BlockSpec(memory_space=pltpu.SMEM) if a.dtype == jnp.int32 else vmem_spec
            for a in args
        ]
    if out_specs is None:
        out_specs = [vmem_spec] * len(outs)
    extra = {} if grid is None else {"grid": grid}
    size = sum(a.size * a.dtype.itemsize for a in args) + sum(
        o.size * o.dtype.itemsize for o in outs
    )
    result = pl.pallas_call(
        kernel,
        out_shape=list(outs),
        in_specs=in_specs,
        out_specs=out_specs,
        scratch_shapes=list(scratch),
        compiler_params=pltpu.CompilerParams(vmem_limit_bytes=vmem * MIB),
        cost_estimate=pl.CostEstimate(flops=flops, bytes_accessed=size, transcendentals=0),
        **extra,
        name=kernel.__name__ if hasattr(kernel, "__name__") else kernel.func.__name__,
    )(*args)
    return result


def like(shape, dtype):
    return jax.ShapeDtypeStruct(shape, dtype)


def project(place, own, n1, n2, n3, x_ref, q_ref, y_ref):
    t = place[0]
    for k, part in enumerate((own, n1, n2, n3)):
        q_ref[t ^ k] = part[...]
    parts, _, width = q_ref.shape
    total = dot(q_ref[0], x_ref[:, :width], contract_last)
    for k in range(1, parts):
        total += dot(q_ref[k], x_ref[:, k * width : (k + 1) * width], contract_last)
    y_ref[...] = total


def error_left(q_ref, e_any, out_ref, e_0, e_1, sems):
    parts, _, width = q_ref.shape
    half = parts // 2

    def place_of(k):
        return (e_0, e_1)[k // half].at[:, pl.ds(k % half * width, width)]

    def load(k):
        return pltpu.make_async_copy(e_any.at[:, pl.ds(k * width, width)], place_of(k), sems.at[k])

    for k in range(parts):
        load(k).start()
    for k in range(parts):
        load(k).wait()
        term = dot(q_ref[k], place_of(k)[...], contract_last)
        if k:
            out_ref[...] += term
        else:
            out_ref[...] = term


def left_factor(place, eq_ref, own, n1, n2, n3, dy_ref, out_ref, y4):
    t = place[0]
    for k, part in enumerate((own, n1, n2, n3)):
        y4[t ^ k] = part[...]
    parts, rank, tokens = y4.shape
    total = eq_ref[...]
    for s in range(parts):
        both = jnp.concatenate(split(y4[s]), axis=0)
        term = dot(both, dy_ref[s * tokens : (s + 1) * tokens, :])
        total += term[:rank] + term[rank:]
    out_ref[...] = total.astype(bf16)


def first_partner(t):
    return jnp.where((t == 1) | (t == 2), 2, 1)


def weigh(place, own, n1, n2, n3, dy_ref, p_ref, gram_ref, near_ref, far_ref, held):
    t = place[0]
    p = (own[...].astype(f32) + n1[...].astype(f32)) + (n2[...].astype(f32) + n3[...].astype(f32))
    p = p.astype(bf16)
    p_ref[...] = p
    parts, _, tokens = held.shape
    gram_ref[...] = dot(p, p, contract_last)
    for s in range(parts):
        held[s] = dot(p, dy_ref[s * tokens : (s + 1) * tokens, :], contract_last)
    step = first_partner(t)
    near_ref[0] = held[t]
    near_ref[1] = held[t ^ step]
    far_ref[0] = held[t ^ 3]
    far_ref[1] = held[t ^ 3 ^ step]


def error_right(p_ref, e_0, e_1, out_ref):
    width = e_0.shape[1]
    step = 640
    for k, e_ref in enumerate((e_0, e_1)):
        for c in range(0, width, step):
            out_ref[:, k * width + c : k * width + c + step] = dot(p_ref[...], e_ref[:, c : c + step])


def right_term(place, near_ref, got_ref, te_ref, x_own, x_first, keep_ref, send_ref, held):
    core = place[1]
    rank = te_ref.shape[0]
    total = te_ref[...]
    for k, x_ref in enumerate((x_own, x_first)):
        both = jnp.concatenate(split(near_ref[k] + got_ref[k]), axis=0)
        term = dot(both, x_ref[...])
        total += term[:rank] + term[rank:]
    held[0] = total[: rank // 2]
    held[1] = total[rank // 2 :]
    keep_ref[...] = held[core]
    send_ref[...] = held[1 - core]


def cut(place, keep, got, o0, o1, o2, o3, held):
    chip = place[2]
    total = keep[...] + got[...]
    width = held.shape[2]
    for s in range(held.shape[0]):
        held[s] = total[:, s * width : (s + 1) * width]
    for k, out in enumerate((o0, o1, o2, o3)):
        out[...] = held[chip ^ k]


def pack(a, b, c, d, gram_ref, out_ref):
    half, width = a.shape
    rank = 2 * half
    out_ref[...] = jnp.zeros_like(out_ref)
    out_ref[:, :width] = (a[...] + b[...]) + (c[...] + d[...])
    out_ref[:, width : width + rank] = gram_ref[:half, :]
    out_ref[:, width + 128 : width + 128 + rank] = gram_ref[half:, :]


def unpack(a, b, c, d, out_ref, gram_ref):
    half, width = out_ref.shape
    rank = 2 * half
    total = (a[...] + b[...]) + (c[...] + d[...])
    out_ref[...] = total[:, :width]
    gram_ref[:half, :] = total[:, width : width + rank]
    gram_ref[half:, :] = total[:, width + 128 : width + 128 + rank]


def invert_cholesky(g_ref, out_ref):
    n = g_ref.shape[0]
    rows = lax.broadcasted_iota(jnp.int32, (n, n), 0)
    cols = lax.broadcasted_iota(jnp.int32, (n, n), 1)
    a = g_ref[...]
    inverse = jnp.where(rows == cols, 1.0, 0.0).astype(f32)
    for j in range(n):
        column = jnp.sum(jnp.where(cols == j, a, 0.0), axis=1, keepdims=True)
        pivot = column[j : j + 1, :]
        factor = jnp.where(rows[:, :1] > j, column / pivot, 0.0)
        a = a - factor * a[j : j + 1, :]
        inverse = inverse - factor * inverse[j : j + 1, :]
    diagonal = jnp.sum(jnp.where(rows == cols, a, 0.0), axis=1, keepdims=True)
    out_ref[...] = inverse * lax.rsqrt(diagonal)


def arrange(place, dy_ref, main_ref, rest_ref, held):
    t = place[0]
    step = first_partner(t)
    tokens = rest_ref.shape[1]
    for k, source in enumerate((t, t ^ step, t ^ 3 ^ step, t ^ 3)):
        held[k * tokens : (k + 1) * tokens, :] = dy_ref[pl.ds(pl.multiple_of(source * tokens, tokens), tokens), :]
    main = main_ref.shape[1]
    main_ref[...] = held[:main, :].T
    rest_ref[...] = held[main:, :].T


def accumulate(first, main_ref, e_ref, x_own, x_first, x_second, acc_ref, x_ref, sems):
    width = acc_ref.shape[1]
    rows = x_own.shape[0]
    copies = [
        pltpu.make_async_copy(source.at[:, pl.ds(first, width)], x_ref.at[pl.ds(k * rows, rows), :], sems.at[k])
        for k, source in enumerate((x_own, x_first, x_second))
    ]
    for copy in copies:
        copy.start()
    for copy in copies:
        copy.wait()
    step, block = 640, 432
    for c in range(0, width, step):
        cols = slice(c, c + step)
        for r in range(0, acc_ref.shape[0], block):
            at = slice(r, r + block)
            acc_ref[at, cols] = dot(main_ref[at, :], x_ref[:, cols]) + e_ref[at, cols].astype(f32)


def finish(replicas, place, linv, p_ref, rest_ref, a0, a1, a2, a3, b0, b1, b2, b3, new_ref, left_ref, right_ref, held, nf4):
    t, core, chip = place[0], place[1], place[2]
    for k, (a, b) in enumerate(((a0, b0), (a1, b1), (a2, b2), (a3, b3))):
        held[chip ^ k, core] = a[...]
        held[chip ^ k, 1 - core] = b[...]
    highest = lax.Precision.HIGHEST
    parts, _, half, width = held.shape
    rank = 2 * half
    scaled = linv[...] * (1.0 / replicas)
    for s in range(parts):
        nf = dot(scaled, held[s].reshape(rank, width), precision=highest)
        nf4[s] = nf
        high, low = split(nf)
        at = slice(s * width, (s + 1) * width)
        right_ref[:rank, at] = high
        right_ref[rank : 2 * rank, at] = high
        right_ref[2 * rank :, at] = low
    new_ref[...] = nf4[t]
    basis = dot(linv[...], p_ref[...].astype(f32), precision=highest)
    high, low = split(-basis)
    base = rest_ref.shape[1]
    left_ref[:, :base] = rest_ref[...]
    left_ref[:, base:] = jnp.concatenate((high, low, high), axis=0).T


def rebuild(place, left_ref, right_ref, acc_0, acc_1, outer, inner, out_any, buffer, staged, sems, out_sems):
    t = place[0]
    rows = inner.shape[0]
    is_inner = (t == 1) | (t == 2)

    def fetch(source):
        return pltpu.make_async_copy(source, buffer.at[pl.ds(0, rows), :], sems.at[0])

    @pl.when(is_inner)
    def _():
        fetch(inner).start()

    @pl.when(jnp.logical_not(is_inner))
    def _():
        fetch(outer).start()

    buffer[rows:, :] = right_ref[...]
    fetch(inner).wait()
    width = staged.shape[2]
    count = acc_0.shape[1] // width

    def put(i, slot):
        return pltpu.make_async_copy(staged.at[slot], out_any.at[:, pl.ds(pl.multiple_of(i * width, width), width)], out_sems.at[slot])

    for part, acc_ref in enumerate((acc_0, acc_1)):

        @pl.loop(0, count)
        def _(c):
            i = part * count + c
            slot = lax.rem(i, 2)

            @pl.when(i >= 2)
            def _():
                put(i - 2, slot).wait()

            here = pl.ds(pl.multiple_of(c * width, width), width)
            cols = pl.ds(pl.multiple_of(i * width, width), width)
            block = 432
            for r in range(0, acc_ref.shape[0], block):
                at = slice(r, r + block)
                total = acc_ref[at, here] + dot(left_ref[at, :], buffer[:, cols])
                staged[slot, at, :] = total.astype(bf16)
            put(i, slot).start()

    for i in (2 * count - 2, 2 * count - 1):
        put(i, i % 2).wait()


def after(value, *others):
    return lax.optimization_barrier((value, *others))[0]


def partners(value, axis, size, by):
    return [lax.ppermute(value, axis, [(i, i ^ k) for i in range(size)]) for k in by]


def body(activations, out_grad, error_state, right_factor):
    errors = error_state[0]
    n_dp, n_t = lax.axis_size("dp"), lax.axis_size("tensor")
    rows, rank = right_factor.shape
    tokens, features = activations.shape
    all_tokens, hidden = out_grad.shape
    half = rank // 2
    t, d = lax.axis_index("tensor"), lax.axis_index("dp")
    place = jnp.stack([t, d & 1, d >> 1]).astype(jnp.int32)
    along_t = functools.partial(partners, axis="tensor", size=n_t, by=(1, 2, 3))
    along_xy = functools.partial(partners, axis="dp", size=n_dp, by=(2, 4, 6))

    anywhere = pl.BlockSpec(memory_space=pl.ANY)
    vmem_spec = pl.BlockSpec(memory_space=pltpu.VMEM)
    smem_spec = pl.BlockSpec(memory_space=pltpu.SMEM)
    hbm_spec = pl.BlockSpec(memory_space=pltpu.HBM)

    def move(value, perm, *when):
        return lax.ppermute(after(value, *when), "tensor", perm)

    q_own = right_factor.T.astype(bf16)
    q_parts = along_t(q_own)

    main = 3 * tokens
    main_t, rest_t = call(
        arrange,
        [like((hidden, main), bf16), like((hidden, all_tokens - main), bf16)],
        place, out_grad,
        scratch=[pltpu.VMEM((all_tokens, hidden), bf16)],
    )
    q_parts, _ = lax.optimization_barrier((q_parts, main_t))
    way_1, way_2 = [(0, 2), (2, 3), (3, 1), (1, 0)], [(0, 1), (1, 3), (3, 2), (2, 0)]
    q_full, y_own = call(
        project,
        [like((n_t, rank, rows), bf16), like((rank, tokens), f32)],
        place, q_own, *q_parts, activations,
    )
    y_parts = along_t(y_own)
    eq, *held_errors = call(
        error_left,
        [like((rank, hidden), f32)] + [like((hidden, features // 2), bf16)] * 2,
        q_full, errors,
        in_specs=[vmem_spec, hbm_spec],
        scratch=[pltpu.SemaphoreType.DMA((n_t,))],
        vmem=40,
    )
    y_parts[0] = after(y_parts[0], eq)
    x_first = move(activations, way_1, *y_parts)
    (p_local,) = call(
        left_factor,
        [like((rank, hidden), bf16)],
        place, eq, y_own, *y_parts, out_grad,
        flops=KA,
        scratch=[pltpu.VMEM((n_t, rank, tokens), f32)],
    )
    (p_other,) = partners(p_local, "dp", n_dp, (1,))
    p_chip = (p_local.astype(f32) + p_other.astype(f32)).astype(bf16)
    p_parts = along_xy(p_chip)
    p_parts[0] = after(p_parts[0], x_first)
    p_total, gram, near_w, far_w = call(
        weigh,
        [like((rank, hidden), bf16), like((rank, rank), f32), like((2, rank, tokens), f32), like((2, rank, tokens), f32)],
        place, p_chip, *p_parts, out_grad,
        scratch=[pltpu.VMEM((n_t, rank, tokens), f32)],
    )
    (got_w,) = partners(far_w, "tensor", n_t, (3,))
    (te,) = call(error_right, [like((rank, features), f32)], p_total, *held_errors)
    got_w = after(got_w, te)
    keep, given = call(
        right_term,
        [like((half, features), f32), like((half, features), f32)],
        place, near_w, got_w, te, activations, x_first,
        scratch=[pltpu.VMEM((2, half, features), f32)],
    )
    x_second = move(activations, way_2, p_total)
    got_w = after(got_w, te)
    keep, given = call(
        right_term,
        [like((half, features), f32), like((half, features), f32)],
        place, near_w, got_w, te, activations, x_first,
        scratch=[pltpu.VMEM((2, half, features), f32)],
    )
    cut_at = tokens // 32 * 16 + 16
    to_outer, to_inner = [], []

    def third_step(part, *when):
        to_outer.append(move(x_first[part], [(1, 0), (2, 3)], *when))
        to_inner.append(move(activations[part], [(1, 2), (2, 1)], *when))

    third_step(slice(0, cut_at), got_w)
    (got,) = partners(given, "dp", n_dp, (1,))
    parts = call(
        cut,
        [like((half, rows), f32)] * 4,
        place, keep, got,
        flops=KB,
        scratch=[pltpu.VMEM((n_t, half, rows), f32)],
    )
    arrived = [
        lax.ppermute(m, "dp", [(i, i ^ (2 * k)) for i in range(n_dp)])
        for k, m in enumerate(parts)
        if k
    ]
    accs = []
    for k, e_held in enumerate(held_errors):
        accs += call(
            functools.partial(accumulate, k * (features // 2)),
            [like((hidden, features // 2), f32)],
            main_t, e_held, activations, x_first, x_second,
            flops=KP,
            in_specs=[vmem_spec, vmem_spec] + [anywhere] * 3,
            scratch=[pltpu.VMEM((main, features // 2), bf16), pltpu.SemaphoreType.DMA((3,))],
        )
    (mine,) = call(pack, [like((half, rows + 256), f32)], parts[0], *arrived, gram)
    mine = after(mine, x_second)
    z1, z2, z3 = along_t(mine)
    x_outer = move(x_first, [(1, 0), (2, 3)], mine)
    x_inner = move(activations, [(1, 2), (2, 1)], mine)
    mine, gram = call(unpack, [like((half, rows), f32), like((rank, rank), f32)], mine, z1, z2, z3)
    (linv,) = call(invert_cholesky, [like((rank, rank), f32)], gram)
    near = [mine] + along_xy(mine)
    near[1] = after(near[1], linv)
    far = [partners(v, "dp", n_dp, (1,))[0] for v in near]
    new_factor, left, right = call(
        functools.partial(finish, n_dp),
        [like((rank, rows), f32), like((hidden, tokens + 3 * rank), bf16), like((3 * rank, features), bf16)],
        place, linv, p_total, rest_t, *near, *far,
        scratch=[pltpu.VMEM((4, 2, half, rows), f32), pltpu.VMEM((n_t, rank, rows), f32)],
    )
    (new_error,) = call(
        rebuild,
        [like((hidden, features), bf16)],
        place, left, right, *accs, x_outer, x_inner,
        in_specs=[smem_spec] + [vmem_spec] * 4 + [anywhere] * 2,
        out_specs=[anywhere],
        scratch=[
            pltpu.VMEM((tokens + 3 * rank, features), bf16),
            pltpu.VMEM((2, hidden, 640), bf16),
            pltpu.SemaphoreType.DMA((1,)),
            pltpu.SemaphoreType.DMA((2,)),
        ],
    )
    return (new_error[None], new_factor.T)


def solution(mesh):
    placed = (
        P(("dp", "tensor"), None),
        P("dp", "tensor"),
        P("dp", "tensor", None),
        P("tensor", None),
    )
    fits = mesh.shape["dp"] == 8 and mesh.shape["tensor"] == 4
    return jax.shard_map(
        body if fits else plain_body,
        mesh=mesh,
        in_specs=placed,
        out_specs=(P("dp", "tensor", None), P("tensor", None)),
        check_vma=False,
    )
```

```python
import functools
import jax
import jax.numpy as jnp
from jax import lax
from jax.experimental import pallas as pl
from jax.experimental.pallas import tpu as pltpu
from jax.sharding import PartitionSpec as P

contract_first = (((0,), (0,)), ((), ()))
contract_last = (((1,), (1,)), ((), ()))
column_block = 8
bf16, f32 = jnp.bfloat16, jnp.float32
MIB = 1 << 20
KA, KB, KP = 0, 3_900_000_000, 3_500_000_000


def plain_body(activations, out_grad, error_state, right_factor):
    highest = lax.Precision.HIGHEST
    errors = error_state[0]
    rows_here = right_factor.shape[0]
    factor_full = lax.all_gather(right_factor, "tensor", axis=0, tiled=True)
    grad = lax.dot_general(
        out_grad,
        lax.all_gather(activations, "tensor", axis=0, tiled=True),
        contract_first,
        preferred_element_type=f32,
    )
    corrected = grad + errors.astype(f32)
    p_local = jnp.dot(corrected, factor_full, precision=highest)
    p_total = lax.psum(p_local.astype(bf16), "dp").astype(f32)
    p_basis = jnp.zeros_like(p_total)
    for block_index in range(p_total.shape[1] // column_block):
        first = block_index * column_block
        columns = p_total[:, first : first + column_block]
        coeffs, block_gram = lax.psum(
            (
                jnp.dot(p_basis.T, columns, precision=highest),
                jnp.dot(columns.T, columns, precision=highest),
            ),
            "tensor",
        )
        remainder = columns - jnp.dot(p_basis, coeffs, precision=highest)
        residual_gram = block_gram - jnp.dot(coeffs.T, coeffs, precision=highest)
        lower_factor = jnp.linalg.cholesky(residual_gram)
        orthonormal = lax.linalg.triangular_solve(
            lower_factor, remainder, left_side=False, lower=True, transpose_a=True
        )
        p_basis = p_basis.at[:, first : first + column_block].set(orthonormal)
    replicas = lax.axis_size("dp")
    term = lax.dot_general(corrected, p_basis, contract_first, precision=highest)
    summed = lax.psum(term, ("dp", "tensor")) / replicas
    new_error = (corrected - jnp.dot(p_basis, summed.T, precision=highest)).astype(bf16)
    new_factor = lax.dynamic_slice_in_dim(
        summed, lax.axis_index("tensor") * rows_here, rows_here, 0
    )
    return (new_error[None], new_factor)


def dot(a, b, dims=None, precision=None):
    if dims is None:
        dims = (((1,), (0,)), ((), ()))
    return lax.dot_general(a, b, dims, precision=precision, preferred_element_type=f32)


def split(v):
    high = v.astype(bf16)
    return high, (v - high.astype(f32)).astype(bf16)


def call(kernel, outs, *args, scratch=(), grid=None, in_specs=None, out_specs=None, vmem=8, flops=0, moved=0):
    vmem_spec = pl.BlockSpec(memory_space=pltpu.VMEM)
    if in_specs is None:
        in_specs = [
            pl.BlockSpec(memory_space=pltpu.SMEM) if a.dtype == jnp.int32 else vmem_spec
            for a in args
        ]
    if out_specs is None:
        out_specs = [vmem_spec] * len(outs)
    extra = {} if grid is None else {"grid": grid}
    size = sum(a.size * a.dtype.itemsize for a in args) + sum(
        o.size * o.dtype.itemsize for o in outs
    )
    result = pl.pallas_call(
        kernel,
        out_shape=list(outs),
        in_specs=in_specs,
        out_specs=out_specs,
        scratch_shapes=list(scratch),
        compiler_params=pltpu.CompilerParams(vmem_limit_bytes=vmem * MIB),
        cost_estimate=pl.CostEstimate(flops=flops, bytes_accessed=size, transcendentals=0),
        **extra,
        name=kernel.__name__ if hasattr(kernel, "__name__") else kernel.func.__name__,
    )(*args)
    return result


def like(shape, dtype):
    return jax.ShapeDtypeStruct(shape, dtype)


def project(place, own, n1, n2, n3, x_ref, q_ref, y_ref):
    t = place[0]
    for k, part in enumerate((own, n1, n2, n3)):
        q_ref[t ^ k] = part[...]
    parts, _, width = q_ref.shape
    total = dot(q_ref[0], x_ref[:, :width], contract_last)
    for k in range(1, parts):
        total += dot(q_ref[k], x_ref[:, k * width : (k + 1) * width], contract_last)
    y_ref[...] = total


def error_left(q_ref, e_any, out_ref, e_0, e_1, sems):
    parts, _, width = q_ref.shape
    half = parts // 2

    def place_of(k):
        return (e_0, e_1)[k // half].at[:, pl.ds(k % half * width, width)]

    def load(k):
        return pltpu.make_async_copy(e_any.at[:, pl.ds(k * width, width)], place_of(k), sems.at[k])

    for k in range(parts):
        load(k).start()
    for k in range(parts):
        load(k).wait()
        term = dot(q_ref[k], place_of(k)[...], contract_last)
        if k:
            out_ref[...] += term
        else:
            out_ref[...] = term


def left_factor(place, eq_ref, own, n1, n2, n3, dy_ref, out_ref, y4):
    t = place[0]
    for k, part in enumerate((own, n1, n2, n3)):
        y4[t ^ k] = part[...]
    parts, rank, tokens = y4.shape
    total = eq_ref[...]
    for s in range(parts):
        both = jnp.concatenate(split(y4[s]), axis=0)
        term = dot(both, dy_ref[s * tokens : (s + 1) * tokens, :])
        total += term[:rank] + term[rank:]
    out_ref[...] = total.astype(bf16)


def first_partner(t):
    return jnp.where((t == 1) | (t == 2), 2, 1)


def weigh(place, own, n1, n2, n3, dy_ref, p_ref, gram_ref, near_ref, far_ref, held):
    t = place[0]
    p = (own[...].astype(f32) + n1[...].astype(f32)) + (n2[...].astype(f32) + n3[...].astype(f32))
    p = p.astype(bf16)
    p_ref[...] = p
    parts, _, tokens = held.shape
    gram_ref[...] = dot(p, p, contract_last)
    for s in range(parts):
        held[s] = dot(p, dy_ref[s * tokens : (s + 1) * tokens, :], contract_last)
    step = first_partner(t)
    near_ref[0] = held[t]
    near_ref[1] = held[t ^ step]
    far_ref[0] = held[t ^ 3]
    far_ref[1] = held[t ^ 3 ^ step]


def error_right(p_ref, e_0, e_1, out_ref):
    width = e_0.shape[1]
    step = 640
    for k, e_ref in enumerate((e_0, e_1)):
        for c in range(0, width, step):
            out_ref[:, k * width + c : k * width + c + step] = dot(p_ref[...], e_ref[:, c : c + step])


def right_term(place, near_ref, got_ref, te_ref, x_own, x_first, keep_ref, send_ref, held):
    core = place[1]
    rank = te_ref.shape[0]
    total = te_ref[...]
    for k, x_ref in enumerate((x_own, x_first)):
        both = jnp.concatenate(split(near_ref[k] + got_ref[k]), axis=0)
        term = dot(both, x_ref[...])
        total += term[:rank] + term[rank:]
    held[0] = total[: rank // 2]
    held[1] = total[rank // 2 :]
    keep_ref[...] = held[core]
    send_ref[...] = held[1 - core]


def cut(place, keep, got, o0, o1, o2, o3, held):
    chip = place[2]
    total = keep[...] + got[...]
    width = held.shape[2]
    for s in range(held.shape[0]):
        held[s] = total[:, s * width : (s + 1) * width]
    for k, out in enumerate((o0, o1, o2, o3)):
        out[...] = held[chip ^ k]


def pack(a, b, c, d, gram_ref, out_ref):
    half, width = a.shape
    rank = 2 * half
    out_ref[...] = jnp.zeros_like(out_ref)
    out_ref[:, :width] = (a[...] + b[...]) + (c[...] + d[...])
    out_ref[:, width : width + rank] = gram_ref[:half, :]
    out_ref[:, width + 128 : width + 128 + rank] = gram_ref[half:, :]


def unpack(a, b, c, d, out_ref, gram_ref):
    half, width = out_ref.shape
    rank = 2 * half
    total = (a[...] + b[...]) + (c[...] + d[...])
    out_ref[...] = total[:, :width]
    gram_ref[:half, :] = total[:, width : width + rank]
    gram_ref[half:, :] = total[:, width + 128 : width + 128 + rank]


def invert_cholesky(g_ref, out_ref):
    n = g_ref.shape[0]
    rows = lax.broadcasted_iota(jnp.int32, (n, n), 0)
    cols = lax.broadcasted_iota(jnp.int32, (n, n), 1)
    a = g_ref[...]
    inverse = jnp.where(rows == cols, 1.0, 0.0).astype(f32)
    for j in range(0, n, 2):
        first = jnp.sum(jnp.where(cols == j, a, 0.0), axis=1, keepdims=True)
        second = jnp.sum(jnp.where(cols == j + 1, a, 0.0), axis=1, keepdims=True)
        row, row_inverse = a[j : j + 1, :], inverse[j : j + 1, :]
        factor = jnp.where(rows[:, :1] > j, first / first[j : j + 1, :], 0.0)
        step = factor[j + 1 : j + 2, :]
        next_row = a[j + 1 : j + 2, :] - step * row
        next_inverse = inverse[j + 1 : j + 2, :] - step * row_inverse
        second = second - factor * first[j + 1 : j + 2, :]
        next_factor = jnp.where(rows[:, :1] > j + 1, second / second[j + 1 : j + 2, :], 0.0)
        a = a - factor * row - next_factor * next_row
        inverse = inverse - factor * row_inverse - next_factor * next_inverse
    diagonal = jnp.sum(jnp.where(rows == cols, a, 0.0), axis=1, keepdims=True)
    out_ref[...] = inverse * lax.rsqrt(diagonal)


def arrange(place, dy_ref, main_ref, rest_ref, held):
    t = place[0]
    step = first_partner(t)
    tokens = rest_ref.shape[1]
    for k, source in enumerate((t, t ^ step, t ^ 3 ^ step, t ^ 3)):
        held[k * tokens : (k + 1) * tokens, :] = dy_ref[pl.ds(pl.multiple_of(source * tokens, tokens), tokens), :]
    main = main_ref.shape[1]
    main_ref[...] = held[:main, :].T
    rest_ref[...] = held[main:, :].T


def accumulate(first, lane, spans, main_ref, base_ref, *rest):
    sources, (acc_ref, x_ref, sems) = rest[: len(spans)], rest[len(spans) :]
    width = acc_ref.shape[1]
    copies, at = [], 0
    for k, (source, (begin, end)) in enumerate(zip(sources, spans)):
        part = source.at[pl.ds(begin, end - begin), pl.ds(first, width)]
        copies.append(pltpu.make_async_copy(part, x_ref.at[pl.ds(at, end - begin), :], sems.at[k]))
        at += end - begin
    for copy in copies:
        copy.start()
    for copy in copies:
        copy.wait()
    step, block = 256, acc_ref.shape[0] // 4
    for c in range(0, width, step):
        cols = slice(c, c + step)
        for r in range(0, acc_ref.shape[0], block):
            here = slice(r, r + block)
            term = dot(main_ref[here, lane : lane + at], x_ref[:, cols])
            acc_ref[here, cols] = term + base_ref[here, cols].astype(f32)


def finish(replicas, place, linv, p_ref, rest_ref, a0, a1, a2, a3, b0, b1, b2, b3, new_ref, left_ref, right_ref, held, nf4):
    t, core, chip = place[0], place[1], place[2]
    for k, (a, b) in enumerate(((a0, b0), (a1, b1), (a2, b2), (a3, b3))):
        held[chip ^ k, core] = a[...]
        held[chip ^ k, 1 - core] = b[...]
    parts, _, half, width = held.shape
    rank = 2 * half
    l_high, l_low = split(linv[...])
    both = jnp.concatenate((l_high, l_low), axis=0)
    for s in range(parts):
        t_high, t_low = split(held[s].reshape(rank, width))
        term = dot(both, t_high)
        nf = (term[:rank] + (term[rank:] + dot(l_high, t_low))) * (1.0 / replicas)
        nf4[s] = nf
        high, low = split(nf)
        at = slice(s * width, (s + 1) * width)
        right_ref[:rank, at] = high
        right_ref[rank : 2 * rank, at] = high
        right_ref[2 * rank :, at] = low
    new_ref[...] = nf4[t]
    term = dot(both, p_ref[...])
    high, low = split(-(term[:rank] + term[rank:]))
    base = rest_ref.shape[1]
    left_ref[:, :base] = rest_ref[...]
    left_ref[:, base:] = jnp.concatenate((high, low, high), axis=0).T


def rebuild(place, left_ref, right_ref, acc_0, acc_1, outer, inner, out_any, buffer, staged, sems, out_sems):
    t = place[0]
    rows = inner.shape[0]
    is_inner = (t == 1) | (t == 2)

    def fetch(source):
        return pltpu.make_async_copy(source, buffer.at[pl.ds(0, rows), :], sems.at[0])

    @pl.when(is_inner)
    def _():
        fetch(inner).start()

    @pl.when(jnp.logical_not(is_inner))
    def _():
        fetch(outer).start()

    buffer[rows:, :] = right_ref[...]
    fetch(inner).wait()
    slots, hidden, width = staged.shape
    count = acc_0.shape[1] // width

    def put(i):
        columns = out_any.at[:, pl.ds(i * width, width)]
        return pltpu.make_async_copy(staged.at[i % slots], columns, out_sems.at[i % slots])

    block = hidden // 4
    for i in range(2 * count):
        if i >= slots:
            put(i - slots).wait()
        acc_ref, first = (acc_0, acc_1)[i // count], i % count * width
        for r in range(0, hidden, block):
            at = slice(r, r + block)
            total = acc_ref[at, first : first + width] + dot(left_ref[at, :], buffer[:, i * width : (i + 1) * width])
            staged[i % slots, at, :] = total.astype(bf16)
        put(i).start()
    for i in range(2 * count - slots, 2 * count):
        put(i).wait()


def after(value, *others):
    return lax.optimization_barrier((value, *others))[0]


def partners(value, axis, size, by):
    return [lax.ppermute(value, axis, [(i, i ^ k) for i in range(size)]) for k in by]


def body(activations, out_grad, error_state, right_factor):
    errors = error_state[0]
    n_dp, n_t = lax.axis_size("dp"), lax.axis_size("tensor")
    rows, rank = right_factor.shape
    tokens, features = activations.shape
    all_tokens, hidden = out_grad.shape
    half = rank // 2
    t, d = lax.axis_index("tensor"), lax.axis_index("dp")
    place = jnp.stack([t, d & 1, d >> 1]).astype(jnp.int32)
    along_t = functools.partial(partners, axis="tensor", size=n_t, by=(1, 2, 3))
    along_xy = functools.partial(partners, axis="dp", size=n_dp, by=(2, 4, 6))

    anywhere = pl.BlockSpec(memory_space=pl.ANY)
    vmem_spec = pl.BlockSpec(memory_space=pltpu.VMEM)
    smem_spec = pl.BlockSpec(memory_space=pltpu.SMEM)
    hbm_spec = pl.BlockSpec(memory_space=pltpu.HBM)

    def move(value, perm, *when):
        return lax.ppermute(after(value, *when), "tensor", perm)

    q_own = right_factor.T.astype(bf16)
    q_parts = along_t(q_own)

    main = 3 * tokens
    main_t, rest_t = call(
        arrange,
        [like((hidden, main), bf16), like((hidden, all_tokens - main), bf16)],
        place, out_grad,
        scratch=[pltpu.VMEM((all_tokens, hidden), bf16)],
    )
    q_parts, _ = lax.optimization_barrier((q_parts, main_t))
    way_1, way_2 = [(0, 2), (2, 3), (3, 1), (1, 0)], [(0, 1), (1, 3), (3, 2), (2, 0)]
    q_full, y_own = call(
        project,
        [like((n_t, rank, rows), bf16), like((rank, tokens), f32)],
        place, q_own, *q_parts, activations,
    )
    y_parts = along_t(y_own)
    eq, *held_errors = call(
        error_left,
        [like((rank, hidden), f32)] + [like((hidden, features // 2), bf16)] * 2,
        q_full, errors,
        in_specs=[vmem_spec, hbm_spec],
        scratch=[pltpu.SemaphoreType.DMA((n_t,))],
        vmem=40,
    )
    y_parts[0] = after(y_parts[0], eq)
    x_first = move(activations, way_1, *y_parts)
    (p_local,) = call(
        left_factor,
        [like((rank, hidden), bf16)],
        place, eq, y_own, *y_parts, out_grad,
        flops=KA,
        scratch=[pltpu.VMEM((n_t, rank, tokens), f32)],
    )
    (p_other,) = partners(p_local, "dp", n_dp, (1,))
    p_chip = (p_local.astype(f32) + p_other.astype(f32)).astype(bf16)
    p_parts = along_xy(p_chip)
    p_total, gram, near_w, far_w = call(
        weigh,
        [like((rank, hidden), bf16), like((rank, rank), f32), like((2, rank, tokens), f32), like((2, rank, tokens), f32)],
        place, p_chip, *p_parts, out_grad,
        scratch=[pltpu.VMEM((n_t, rank, tokens), f32)],
    )
    (got_w,) = partners(far_w, "tensor", n_t, (3,))
    (te,) = call(error_right, [like((rank, features), f32)], p_total, *held_errors)
    got_w = after(got_w, te)
    keep, given = call(
        right_term,
        [like((half, features), f32), like((half, features), f32)],
        place, near_w, got_w, te, activations, x_first,
        scratch=[pltpu.VMEM((2, half, features), f32)],
    )
    x_second = move(activations, way_2, p_total)
    got_w = after(got_w, te)
    keep, given = call(
        right_term,
        [like((half, features), f32), like((half, features), f32)],
        place, near_w, got_w, te, activations, x_first,
        scratch=[pltpu.VMEM((2, half, features), f32)],
    )
    cut_at = tokens // 32 * 16 + 16
    to_outer, to_inner = [], []

    def third_step(part, *when):
        to_outer.append(move(x_first[part], [(1, 0), (2, 3)], *when))
        to_inner.append(move(activations[part], [(1, 2), (2, 1)], *when))

    third_step(slice(0, cut_at), got_w)
    (got,) = partners(given, "dp", n_dp, (1,))
    parts = call(
        cut,
        [like((half, rows), f32)] * 4,
        place, keep, got,
        flops=KB,
        scratch=[pltpu.VMEM((n_t, half, rows), f32)],
    )
    arrived = [
        lax.ppermute(m, "dp", [(i, i ^ (2 * k)) for i in range(n_dp)])
        for k, m in enumerate(parts)
        if k
    ]
    def add_tokens(k, cost, lane, base, spans, *sources):
        count = sum(end - begin for begin, end in spans)
        return call(
            functools.partial(accumulate, k * (features // 2), lane, spans),
            [like((hidden, features // 2), f32)],
            main_t, base, *sources,
            flops=cost,
            in_specs=[vmem_spec, vmem_spec] + [anywhere] * len(sources),
            scratch=[pltpu.VMEM((count, features // 2), bf16), pltpu.SemaphoreType.DMA((len(spans),))],
        )[0]

    early = 256 - tokens
    accs = [
        add_tokens(k, 0, 0, e_held, ((0, tokens), (0, early)), activations, x_first)
        for k, e_held in enumerate(held_errors)
    ]
    (mine,) = call(pack, [like((half, rows + 256), f32)], parts[0], *arrived, gram)
    mine = after(mine, *accs)
    z1, z2, z3 = along_t(mine)
    x_outer = move(x_first, [(1, 0), (2, 3)], mine)
    x_inner = move(activations, [(1, 2), (2, 1)], mine)
    accs = [
        add_tokens(k, KP, 256, acc, ((early, tokens), (0, tokens)), x_first, x_second)
        for k, acc in enumerate(accs)
    ]
    mine, gram = call(unpack, [like((half, rows), f32), like((rank, rank), f32)], mine, z1, z2, z3)
    (linv,) = call(invert_cholesky, [like((rank, rank), f32)], gram)
    near = [mine] + along_xy(mine)
    near[1] = after(near[1], linv)
    far = [partners(v, "dp", n_dp, (1,))[0] for v in near]
    new_factor, left, right = call(
        functools.partial(finish, n_dp),
        [like((rank, rows), f32), like((hidden, tokens + 3 * rank), bf16), like((3 * rank, features), bf16)],
        place, linv, p_total, rest_t, *near, *far,
        scratch=[pltpu.VMEM((4, 2, half, rows), f32), pltpu.VMEM((n_t, rank, rows), f32)],
    )
    (new_error,) = call(
        rebuild,
        [like((hidden, features), bf16)],
        place, left, right, *accs, x_outer, x_inner,
        in_specs=[smem_spec] + [vmem_spec] * 4 + [anywhere] * 2,
        out_specs=[anywhere],
        scratch=[
            pltpu.VMEM((tokens + 3 * rank, features), bf16),
            pltpu.VMEM((4, hidden, 256), bf16),
            pltpu.SemaphoreType.DMA((1,)),
            pltpu.SemaphoreType.DMA((4,)),
        ],
    )
    return (new_error[None], new_factor.T)


def solution(mesh):
    placed = (
        P(("dp", "tensor"), None),
        P("dp", "tensor"),
        P("dp", "tensor", None),
        P("tensor", None),
    )
    fits = mesh.shape["dp"] == 8 and mesh.shape["tensor"] == 4
    return jax.shard_map(
        body if fits else plain_body,
        mesh=mesh,
        in_specs=placed,
        out_specs=(P("dp", "tensor", None), P("tensor", None)),
        check_vma=False,
    )
```

```python
import functools
import jax
import jax.numpy as jnp
from jax import lax
from jax.experimental import pallas as pl
from jax.experimental.pallas import tpu as pltpu
from jax.sharding import PartitionSpec as P

contract_first = (((0,), (0,)), ((), ()))
contract_last = (((1,), (1,)), ((), ()))
column_block = 8
bf16, f32 = jnp.bfloat16, jnp.float32
MIB = 1 << 20
CUT_COST, ACC_COST = 1_600_000_000, 2_000_000_000


def plain_body(activations, out_grad, error_state, right_factor):
    highest = lax.Precision.HIGHEST
    errors = error_state[0]
    rows_here = right_factor.shape[0]
    factor_full = lax.all_gather(right_factor, "tensor", axis=0, tiled=True)
    grad = lax.dot_general(
        out_grad,
        lax.all_gather(activations, "tensor", axis=0, tiled=True),
        contract_first,
        preferred_element_type=f32,
    )
    corrected = grad + errors.astype(f32)
    p_local = jnp.dot(corrected, factor_full, precision=highest)
    p_total = lax.psum(p_local.astype(bf16), "dp").astype(f32)
    p_basis = jnp.zeros_like(p_total)
    for block_index in range(p_total.shape[1] // column_block):
        first = block_index * column_block
        columns = p_total[:, first : first + column_block]
        coeffs, block_gram = lax.psum(
            (
                jnp.dot(p_basis.T, columns, precision=highest),
                jnp.dot(columns.T, columns, precision=highest),
            ),
            "tensor",
        )
        remainder = columns - jnp.dot(p_basis, coeffs, precision=highest)
        residual_gram = block_gram - jnp.dot(coeffs.T, coeffs, precision=highest)
        lower_factor = jnp.linalg.cholesky(residual_gram)
        orthonormal = lax.linalg.triangular_solve(
            lower_factor, remainder, left_side=False, lower=True, transpose_a=True
        )
        p_basis = p_basis.at[:, first : first + column_block].set(orthonormal)
    replicas = lax.axis_size("dp")
    term = lax.dot_general(corrected, p_basis, contract_first, precision=highest)
    summed = lax.psum(term, ("dp", "tensor")) / replicas
    new_error = (corrected - jnp.dot(p_basis, summed.T, precision=highest)).astype(bf16)
    new_factor = lax.dynamic_slice_in_dim(
        summed, lax.axis_index("tensor") * rows_here, rows_here, 0
    )
    return (new_error[None], new_factor)


def dot(a, b, dims=None, precision=None):
    if dims is None:
        dims = (((1,), (0,)), ((), ()))
    return lax.dot_general(a, b, dims, precision=precision, preferred_element_type=f32)


def split(v):
    high = v.astype(bf16)
    return high, (v - high.astype(f32)).astype(bf16)


def call(kernel, outs, *args, scratch=(), grid=None, in_specs=None, out_specs=None, vmem=8, flops=0, moved=0):
    vmem_spec = pl.BlockSpec(memory_space=pltpu.VMEM)
    if in_specs is None:
        in_specs = [
            pl.BlockSpec(memory_space=pltpu.SMEM) if a.dtype == jnp.int32 else vmem_spec
            for a in args
        ]
    if out_specs is None:
        out_specs = [vmem_spec] * len(outs)
    extra = {} if grid is None else {"grid": grid}
    size = sum(a.size * a.dtype.itemsize for a in args) + sum(
        o.size * o.dtype.itemsize for o in outs
    )
    result = pl.pallas_call(
        kernel,
        out_shape=list(outs),
        in_specs=in_specs,
        out_specs=out_specs,
        scratch_shapes=list(scratch),
        compiler_params=pltpu.CompilerParams(vmem_limit_bytes=vmem * MIB),
        cost_estimate=pl.CostEstimate(flops=flops, bytes_accessed=size, transcendentals=0),
        **extra,
        name=kernel.__name__ if hasattr(kernel, "__name__") else kernel.func.__name__,
    )(*args)
    return result


def like(shape, dtype):
    return jax.ShapeDtypeStruct(shape, dtype)


def project(place, own, n1, n2, n3, x_ref, q_ref, y_ref):
    t = place[0]
    for k, part in enumerate((own, n1, n2, n3)):
        q_ref[t ^ k] = part[...]
    parts, _, width = q_ref.shape
    total = dot(q_ref[0], x_ref[:, :width], contract_last)
    for k in range(1, parts):
        total += dot(q_ref[k], x_ref[:, k * width : (k + 1) * width], contract_last)
    y_ref[...] = total


def error_left(q_ref, e_any, out_ref, e_0, e_1, sems):
    parts, _, width = q_ref.shape
    half = parts // 2

    def place_of(k):
        return (e_0, e_1)[k // half].at[:, pl.ds(k % half * width, width)]

    def load(k):
        return pltpu.make_async_copy(e_any.at[:, pl.ds(k * width, width)], place_of(k), sems.at[k])

    for k in range(parts):
        load(k).start()
    for k in range(parts):
        load(k).wait()
        term = dot(q_ref[k], place_of(k)[...], contract_last)
        if k:
            out_ref[...] += term
        else:
            out_ref[...] = term


def left_factor(place, eq_ref, own, n1, n2, n3, dy_ref, out_ref, y4):
    t = place[0]
    for k, part in enumerate((own, n1, n2, n3)):
        y4[t ^ k] = part[...]
    parts, rank, tokens = y4.shape
    total = eq_ref[...]
    for s in range(parts):
        both = jnp.concatenate(split(y4[s]), axis=0)
        term = dot(both, dy_ref[s * tokens : (s + 1) * tokens, :])
        total += term[:rank] + term[rank:]
    out_ref[...] = total.astype(bf16)


def first_partner(t):
    return jnp.where((t == 1) | (t == 2), 2, 1)


def weigh(place, own, n1, n2, n3, dy_ref, p_ref, gram_ref, near_ref, far_ref, held):
    t = place[0]
    p = (own[...].astype(f32) + n1[...].astype(f32)) + (n2[...].astype(f32) + n3[...].astype(f32))
    p = p.astype(bf16)
    p_ref[...] = p
    parts, _, tokens = held.shape
    gram_ref[...] = dot(p, p, contract_last)
    for s in range(parts):
        held[s] = dot(p, dy_ref[s * tokens : (s + 1) * tokens, :], contract_last)
    step = first_partner(t)
    near_ref[0] = held[t]
    near_ref[1] = held[t ^ step]
    far_ref[0] = held[t ^ 3].astype(bf16)
    far_ref[1] = held[t ^ 3 ^ step].astype(bf16)


def error_right(p_ref, e_0, e_1, out_ref):
    width = e_0.shape[1]
    step = 640
    for k, e_ref in enumerate((e_0, e_1)):
        for c in range(0, width, step):
            out_ref[:, k * width + c : k * width + c + step] = dot(p_ref[...], e_ref[:, c : c + step])


def right_term(place, near_ref, got_ref, te_ref, x_own, x_first, keep_ref, send_ref, held):
    core = place[1]
    rank = te_ref.shape[0]
    total = te_ref[...]
    for k, x_ref in enumerate((x_own, x_first)):
        both = jnp.concatenate(split(near_ref[k] + got_ref[k].astype(f32)), axis=0)
        term = dot(both, x_ref[...])
        total += term[:rank] + term[rank:]
    held[0] = total[: rank // 2]
    held[1] = total[rank // 2 :]
    keep_ref[...] = held[core]
    send_ref[...] = held[1 - core]


def cut(place, keep, got, o0, o1, o2, o3, held):
    chip = place[2]
    total = keep[...] + got[...]
    width = held.shape[2]
    for s in range(held.shape[0]):
        held[s] = total[:, s * width : (s + 1) * width]
    for k, out in enumerate((o0, o1, o2, o3)):
        out[...] = held[chip ^ k].astype(out.dtype)


def pack(a, b, c, d, gram_ref, out_ref):
    half, width = a.shape
    rank = 2 * half
    total = (a[...] + b[...].astype(f32)) + (c[...].astype(f32) + d[...].astype(f32))
    out_ref[:, :width] = total.astype(bf16)
    left = jnp.concatenate((gram_ref[:half, :], gram_ref[half:, :]), axis=1)
    for k in range(3):
        term = left.astype(bf16)
        left = left - term.astype(f32)
        out_ref[:, width + k * 128 : width + k * 128 + 2 * rank] = term


def unpack(a, b, c, d, out_ref, gram_ref):
    half, width = out_ref.shape
    rank = 2 * half

    def part(ref, at, count):
        return ref[:, at : at + count].astype(f32)

    out_ref[...] = (part(a, 0, width) + part(b, 0, width)) + (part(c, 0, width) + part(d, 0, width))
    grams = [sum(part(ref, width + k * 128, 2 * rank) for k in range(3)) for ref in (a, b, c, d)]
    total = (grams[0] + grams[1]) + (grams[2] + grams[3])
    gram_ref[:half, :] = total[:, :rank]
    gram_ref[half:, :] = total[:, rank:]


def invert_cholesky(g_ref, out_ref):
    n = g_ref.shape[0]
    rows = lax.broadcasted_iota(jnp.int32, (n, n), 0)
    cols = lax.broadcasted_iota(jnp.int32, (n, n), 1)
    a = g_ref[...]
    inverse = jnp.where(rows == cols, 1.0, 0.0).astype(f32)
    for j in range(0, n, 2):
        first = jnp.sum(jnp.where(cols == j, a, 0.0), axis=1, keepdims=True)
        second = jnp.sum(jnp.where(cols == j + 1, a, 0.0), axis=1, keepdims=True)
        row, row_inverse = a[j : j + 1, :], inverse[j : j + 1, :]
        factor = jnp.where(rows[:, :1] > j, first / first[j : j + 1, :], 0.0)
        step = factor[j + 1 : j + 2, :]
        next_row = a[j + 1 : j + 2, :] - step * row
        next_inverse = inverse[j + 1 : j + 2, :] - step * row_inverse
        second = second - factor * first[j + 1 : j + 2, :]
        next_factor = jnp.where(rows[:, :1] > j + 1, second / second[j + 1 : j + 2, :], 0.0)
        a = a - factor * row - next_factor * next_row
        inverse = inverse - factor * row_inverse - next_factor * next_inverse
    diagonal = jnp.sum(jnp.where(rows == cols, a, 0.0), axis=1, keepdims=True)
    out_ref[...] = inverse * lax.rsqrt(diagonal)


def arrange(place, dy_ref, main_ref, rest_ref, held):
    t = place[0]
    step = first_partner(t)
    tokens = rest_ref.shape[1]
    for k, source in enumerate((t, t ^ step, t ^ 3 ^ step, t ^ 3)):
        held[k * tokens : (k + 1) * tokens, :] = dy_ref[pl.ds(pl.multiple_of(source * tokens, tokens), tokens), :]
    main = main_ref.shape[1]
    main_ref[...] = held[:main, :].T
    rest_ref[...] = held[main:, :].T


def accumulate(first, lane, spans, main_ref, base_ref, *rest):
    sources, (acc_ref, x_ref, sems) = rest[: len(spans)], rest[len(spans) :]
    width = acc_ref.shape[1]
    copies, at = [], 0
    for k, (source, (begin, end)) in enumerate(zip(sources, spans)):
        part = source.at[pl.ds(begin, end - begin), pl.ds(first, width)]
        copies.append(pltpu.make_async_copy(part, x_ref.at[pl.ds(at, end - begin), :], sems.at[k]))
        at += end - begin
    for copy in copies:
        copy.start()
    for copy in copies:
        copy.wait()
    step, block = 256, acc_ref.shape[0] // 4
    for c in range(0, width, step):
        cols = slice(c, c + step)
        for r in range(0, acc_ref.shape[0], block):
            here = slice(r, r + block)
            term = dot(main_ref[here, lane : lane + at], x_ref[:, cols])
            acc_ref[here, cols] = term + base_ref[here, cols].astype(f32)


def finish(replicas, place, linv, p_ref, rest_ref, a0, a1, a2, a3, b0, b1, b2, b3, new_ref, left_ref, right_ref, held, nf4):
    t, core, chip = place[0], place[1], place[2]
    for k, (a, b) in enumerate(((a0, b0), (a1, b1), (a2, b2), (a3, b3))):
        held[chip ^ k, core] = a[...]
        held[chip ^ k, 1 - core] = b[...]
    parts, _, half, width = held.shape
    rank = 2 * half
    l_high, l_low = split(linv[...])
    both = jnp.concatenate((l_high, l_low), axis=0)
    for s in range(parts):
        t_high, t_low = split(held[s].reshape(rank, width))
        term = dot(both, t_high)
        nf = (term[:rank] + (term[rank:] + dot(l_high, t_low))) * (1.0 / replicas)
        nf4[s] = nf
        high, low = split(nf)
        at = slice(s * width, (s + 1) * width)
        right_ref[:rank, at] = high
        right_ref[rank : 2 * rank, at] = high
        right_ref[2 * rank :, at] = low
    new_ref[...] = nf4[t]
    term = dot(both, p_ref[...])
    high, low = split(-(term[:rank] + term[rank:]))
    base = rest_ref.shape[1]
    left_ref[:, :base] = rest_ref[...]
    left_ref[:, base:] = jnp.concatenate((high, low, high), axis=0).T


def rebuild(left_ref, right_ref, acc_0, acc_1, x_any, out_any, buffer, staged, sem, out_sems):
    rows = x_any.shape[0]
    fetch = pltpu.make_async_copy(x_any, buffer.at[pl.ds(0, rows), :], sem)
    fetch.start()
    buffer[rows:, :] = right_ref[...]
    fetch.wait()
    slots, hidden, width = staged.shape
    count = acc_0.shape[1] // width

    def put(i):
        columns = out_any.at[:, pl.ds(i * width, width)]
        return pltpu.make_async_copy(staged.at[i % slots], columns, out_sems.at[i % slots])

    block = hidden // 4
    for i in range(2 * count):
        if i >= slots:
            put(i - slots).wait()
        acc_ref, first = (acc_0, acc_1)[i // count], i % count * width
        for r in range(0, hidden, block):
            at = slice(r, r + block)
            total = acc_ref[at, first : first + width] + dot(left_ref[at, :], buffer[:, i * width : (i + 1) * width])
            staged[i % slots, at, :] = total.astype(bf16)
        put(i).start()
    for i in range(2 * count - slots, 2 * count):
        put(i).wait()


def after(value, *others):
    return lax.optimization_barrier((value, *others))[0]


def partners(value, axis, size, by):
    return [lax.ppermute(value, axis, [(i, i ^ k) for i in range(size)]) for k in by]


def body(activations, out_grad, error_state, right_factor):
    errors = error_state[0]
    n_dp, n_t = lax.axis_size("dp"), lax.axis_size("tensor")
    rows, rank = right_factor.shape
    tokens, features = activations.shape
    all_tokens, hidden = out_grad.shape
    half = rank // 2
    t, d = lax.axis_index("tensor"), lax.axis_index("dp")
    place = jnp.stack([t, d & 1, d >> 1]).astype(jnp.int32)
    along_t = functools.partial(partners, axis="tensor", size=n_t, by=(1, 2, 3))
    along_xy = functools.partial(partners, axis="dp", size=n_dp, by=(2, 4, 6))

    anywhere = pl.BlockSpec(memory_space=pl.ANY)
    vmem_spec = pl.BlockSpec(memory_space=pltpu.VMEM)
    smem_spec = pl.BlockSpec(memory_space=pltpu.SMEM)
    hbm_spec = pl.BlockSpec(memory_space=pltpu.HBM)

    def move(value, perm, *when):
        return lax.ppermute(after(value, *when), "tensor", perm)

    q_own = right_factor.T.astype(bf16)
    q_parts = along_t(q_own)

    main = 3 * tokens
    main_t, rest_t = call(
        arrange,
        [like((hidden, main), bf16), like((hidden, all_tokens - main), bf16)],
        place, out_grad,
        scratch=[pltpu.VMEM((all_tokens, hidden), bf16)],
    )
    q_parts, _ = lax.optimization_barrier((q_parts, main_t))
    way_1, way_2 = [(0, 2), (2, 3), (3, 1), (1, 0)], [(0, 1), (1, 3), (3, 2), (2, 0)]
    q_full, y_own = call(
        project,
        [like((n_t, rank, rows), bf16), like((rank, tokens), f32)],
        place, q_own, *q_parts, activations,
    )
    y_parts = along_t(y_own)
    eq, *held_errors = call(
        error_left,
        [like((rank, hidden), f32)] + [like((hidden, features // 2), bf16)] * 2,
        q_full, errors,
        in_specs=[vmem_spec, hbm_spec],
        scratch=[pltpu.SemaphoreType.DMA((n_t,))],
        vmem=40,
    )
    y_parts[0] = after(y_parts[0], eq)
    x_first = move(activations, way_1, *y_parts)
    (p_local,) = call(
        left_factor,
        [like((rank, hidden), bf16)],
        place, eq, y_own, *y_parts, out_grad,
        scratch=[pltpu.VMEM((n_t, rank, tokens), f32)],
    )
    (p_other,) = partners(p_local, "dp", n_dp, (1,))
    p_chip = (p_local.astype(f32) + p_other.astype(f32)).astype(bf16)
    p_parts = along_xy(p_chip)
    p_total, gram, near_w, far_w = call(
        weigh,
        [like((rank, hidden), bf16), like((rank, rank), f32), like((2, rank, tokens), f32), like((2, rank, tokens), bf16)],
        place, p_chip, *p_parts, out_grad,
        scratch=[pltpu.VMEM((n_t, rank, tokens), f32)],
    )
    (got_w,) = partners(far_w, "tensor", n_t, (3,))
    (te,) = call(error_right, [like((rank, features), f32)], p_total, *held_errors)
    got_w = after(got_w, te)
    keep, given = call(
        right_term,
        [like((half, features), f32), like((half, features), f32)],
        place, near_w, got_w, te, activations, x_first,
        scratch=[pltpu.VMEM((2, half, features), f32)],
    )
    x_second = move(activations, way_2, p_total)
    got_w = after(got_w, te)
    keep, given = call(
        right_term,
        [like((half, features), f32), like((half, features), f32)],
        place, near_w, got_w, te, activations, x_first,
        scratch=[pltpu.VMEM((2, half, features), f32)],
    )
    (got,) = partners(given, "dp", n_dp, (1,))
    parts = call(
        cut,
        [like((half, rows), f32)] + [like((half, rows), bf16)] * 3,
        place, keep, got,
        flops=CUT_COST,
        scratch=[pltpu.VMEM((n_t, half, rows), f32)],
    )
    arrived = [
        lax.ppermute(m, "dp", [(i, i ^ (2 * k)) for i in range(n_dp)])
        for k, m in enumerate(parts)
        if k
    ]
    def add_tokens(k, cost, lane, base, spans, *sources):
        count = sum(end - begin for begin, end in spans)
        return call(
            functools.partial(accumulate, k * (features // 2), lane, spans),
            [like((hidden, features // 2), f32)],
            main_t, base, *sources,
            flops=cost,
            in_specs=[vmem_spec, vmem_spec] + [anywhere] * len(sources),
            scratch=[pltpu.VMEM((count, features // 2), bf16), pltpu.SemaphoreType.DMA((len(spans),))],
        )[0]

    early = 256 - tokens
    accs = [
        add_tokens(k, 0, 0, e_held, ((0, tokens), (0, early)), activations, x_first)
        for k, e_held in enumerate(held_errors)
    ]
    (mine,) = call(pack, [like((half, rows + 384), bf16)], parts[0], *arrived, gram)
    mine = after(mine, *accs)
    z1, z2, z3 = along_t(mine)
    x_third = move(x_first, way_1, z1, z2, z3)
    accs = [
        add_tokens(k, ACC_COST, 256, acc, ((early, tokens), (0, tokens)), x_first, x_second)
        for k, acc in enumerate(accs)
    ]
    mine, gram = call(unpack, [like((half, rows), f32), like((rank, rank), f32)], mine, z1, z2, z3)
    (linv,) = call(invert_cholesky, [like((rank, rank), f32)], gram)
    near = [mine] + along_xy(mine)
    near[1] = after(near[1], linv)
    far = [partners(v, "dp", n_dp, (1,))[0] for v in near]
    new_factor, left, right = call(
        functools.partial(finish, n_dp),
        [like((rank, rows), f32), like((hidden, tokens + 3 * rank), bf16), like((3 * rank, features), bf16)],
        place, linv, p_total, rest_t, *near, *far,
        scratch=[pltpu.VMEM((4, 2, half, rows), f32), pltpu.VMEM((n_t, rank, rows), f32)],
    )
    (new_error,) = call(
        rebuild,
        [like((hidden, features), bf16)],
        left, right, *accs, x_third,
        in_specs=[vmem_spec] * 4 + [anywhere],
        out_specs=[anywhere],
        scratch=[
            pltpu.VMEM((tokens + 3 * rank, features), bf16),
            pltpu.VMEM((4, hidden, 256), bf16),
            pltpu.SemaphoreType.DMA(()),
            pltpu.SemaphoreType.DMA((4,)),
        ],
    )
    return (new_error[None], new_factor.T)


def solution(mesh):
    placed = (
        P(("dp", "tensor"), None),
        P("dp", "tensor"),
        P("dp", "tensor", None),
        P("tensor", None),
    )
    fits = mesh.shape["dp"] == 8 and mesh.shape["tensor"] == 4
    return jax.shard_map(
        body if fits else plain_body,
        mesh=mesh,
        in_specs=placed,
        out_specs=(P("dp", "tensor", None), P("tensor", None)),
        check_vma=False,
    )
```

```python
import functools
import jax
import jax.numpy as jnp
from jax import lax
from jax.experimental import pallas as pl
from jax.experimental.pallas import tpu as pltpu
from jax.sharding import PartitionSpec as P

contract_first = (((0,), (0,)), ((), ()))
contract_last = (((1,), (1,)), ((), ()))
column_block = 8
bf16, f32 = jnp.bfloat16, jnp.float32
MIB = 1 << 20
CUT_COST, ACC_COST = 1_600_000_000, 2_000_000_000


def plain_body(activations, out_grad, error_state, right_factor):
    highest = lax.Precision.HIGHEST
    errors = error_state[0]
    rows_here = right_factor.shape[0]
    factor_full = lax.all_gather(right_factor, "tensor", axis=0, tiled=True)
    grad = lax.dot_general(
        out_grad,
        lax.all_gather(activations, "tensor", axis=0, tiled=True),
        contract_first,
        preferred_element_type=f32,
    )
    corrected = grad + errors.astype(f32)
    p_local = jnp.dot(corrected, factor_full, precision=highest)
    p_total = lax.psum(p_local.astype(bf16), "dp").astype(f32)
    p_basis = jnp.zeros_like(p_total)
    for block_index in range(p_total.shape[1] // column_block):
        first = block_index * column_block
        columns = p_total[:, first : first + column_block]
        coeffs, block_gram = lax.psum(
            (
                jnp.dot(p_basis.T, columns, precision=highest),
                jnp.dot(columns.T, columns, precision=highest),
            ),
            "tensor",
        )
        remainder = columns - jnp.dot(p_basis, coeffs, precision=highest)
        residual_gram = block_gram - jnp.dot(coeffs.T, coeffs, precision=highest)
        lower_factor = jnp.linalg.cholesky(residual_gram)
        orthonormal = lax.linalg.triangular_solve(
            lower_factor, remainder, left_side=False, lower=True, transpose_a=True
        )
        p_basis = p_basis.at[:, first : first + column_block].set(orthonormal)
    replicas = lax.axis_size("dp")
    term = lax.dot_general(corrected, p_basis, contract_first, precision=highest)
    summed = lax.psum(term, ("dp", "tensor")) / replicas
    new_error = (corrected - jnp.dot(p_basis, summed.T, precision=highest)).astype(bf16)
    new_factor = lax.dynamic_slice_in_dim(
        summed, lax.axis_index("tensor") * rows_here, rows_here, 0
    )
    return (new_error[None], new_factor)


def dot(a, b, dims=None, precision=None):
    if dims is None:
        dims = (((1,), (0,)), ((), ()))
    return lax.dot_general(a, b, dims, precision=precision, preferred_element_type=f32)


def split(v):
    high = v.astype(bf16)
    return high, (v - high.astype(f32)).astype(bf16)


def call(kernel, outs, *args, scratch=(), grid=None, in_specs=None, out_specs=None, vmem=8, flops=0, moved=0):
    vmem_spec = pl.BlockSpec(memory_space=pltpu.VMEM)
    if in_specs is None:
        in_specs = [
            pl.BlockSpec(memory_space=pltpu.SMEM) if a.dtype == jnp.int32 else vmem_spec
            for a in args
        ]
    if out_specs is None:
        out_specs = [vmem_spec] * len(outs)
    extra = {} if grid is None else {"grid": grid}
    size = sum(a.size * a.dtype.itemsize for a in args) + sum(
        o.size * o.dtype.itemsize for o in outs
    )
    result = pl.pallas_call(
        kernel,
        out_shape=list(outs),
        in_specs=in_specs,
        out_specs=out_specs,
        scratch_shapes=list(scratch),
        compiler_params=pltpu.CompilerParams(vmem_limit_bytes=vmem * MIB),
        cost_estimate=pl.CostEstimate(flops=flops, bytes_accessed=size, transcendentals=0),
        **extra,
        name=kernel.__name__ if hasattr(kernel, "__name__") else kernel.func.__name__,
    )(*args)
    return result


def like(shape, dtype):
    return jax.ShapeDtypeStruct(shape, dtype)


def project(place, own, n1, n2, n3, x_ref, q_ref, y_ref):
    t = place[0]
    for k, part in enumerate((own, n1, n2, n3)):
        q_ref[t ^ k] = part[...]
    parts, _, width = q_ref.shape
    total = dot(q_ref[0], x_ref[:, :width], contract_last)
    for k in range(1, parts):
        total += dot(q_ref[k], x_ref[:, k * width : (k + 1) * width], contract_last)
    y_ref[...] = total


def load_half(e_any, e_ref, sem):
    copy = pltpu.make_async_copy(e_any.at[:, pl.ds(0, e_ref.shape[1])], e_ref, sem)
    copy.start()
    copy.wait()


def error_left(q_ref, e_0, e_any, out_ref, e_1, sems):
    parts, _, width = q_ref.shape
    half = parts // 2

    def load(k):
        return pltpu.make_async_copy(
            e_any.at[:, pl.ds((half + k) * width, width)], e_1.at[:, pl.ds(k * width, width)], sems.at[k]
        )

    for k in range(half):
        load(k).start()
    total = dot(q_ref[0], e_0[:, :width], contract_last)
    for k in range(1, half):
        total += dot(q_ref[k], e_0[:, k * width : (k + 1) * width], contract_last)
    for k in range(half):
        load(k).wait()
        total += dot(q_ref[half + k], e_1[:, k * width : (k + 1) * width], contract_last)
    out_ref[...] = total


def left_factor(place, eq_ref, own, n1, n2, n3, dy_ref, out_ref, y4):
    t = place[0]
    for k, part in enumerate((own, n1, n2, n3)):
        y4[t ^ k] = part[...]
    parts, rank, tokens = y4.shape
    total = eq_ref[...]
    for s in range(parts):
        both = jnp.concatenate(split(y4[s]), axis=0)
        term = dot(both, dy_ref[s * tokens : (s + 1) * tokens, :])
        total += term[:rank] + term[rank:]
    out_ref[...] = total.astype(bf16)


def first_partner(t):
    return jnp.where((t == 1) | (t == 2), 2, 1)


def weigh(place, own, n1, n2, n3, dy_ref, p_ref, gram_ref, near_ref, far_ref, held):
    t = place[0]
    p = (own[...].astype(f32) + n1[...].astype(f32)) + (n2[...].astype(f32) + n3[...].astype(f32))
    p = p.astype(bf16)
    p_ref[...] = p
    parts, _, tokens = held.shape
    gram_ref[...] = dot(p, p, contract_last)
    for s in range(parts):
        held[s] = dot(p, dy_ref[s * tokens : (s + 1) * tokens, :], contract_last)
    step = first_partner(t)
    near_ref[0] = held[t]
    near_ref[1] = held[t ^ step]
    far_ref[0] = held[t ^ 3].astype(bf16)
    far_ref[1] = held[t ^ 3 ^ step].astype(bf16)


def error_right(p_ref, e_0, e_1, out_ref):
    width = e_0.shape[1]
    step = 640
    for k, e_ref in enumerate((e_0, e_1)):
        for c in range(0, width, step):
            out_ref[:, k * width + c : k * width + c + step] = dot(p_ref[...], e_ref[:, c : c + step])


def right_term(place, near_ref, got_ref, te_ref, x_own, x_first, keep_ref, send_ref, held):
    core = place[1]
    rank = te_ref.shape[0]
    total = te_ref[...]
    for k, x_ref in enumerate((x_own, x_first)):
        both = jnp.concatenate(split(near_ref[k] + got_ref[k].astype(f32)), axis=0)
        term = dot(both, x_ref[...])
        total += term[:rank] + term[rank:]
    held[0] = total[: rank // 2]
    held[1] = total[rank // 2 :]
    keep_ref[...] = held[core]
    send_ref[...] = held[1 - core]


def cut(place, keep, got, o0, o1, o2, o3, held):
    chip = place[2]
    total = keep[...] + got[...]
    width = held.shape[2]
    for s in range(held.shape[0]):
        held[s] = total[:, s * width : (s + 1) * width]
    for k, out in enumerate((o0, o1, o2, o3)):
        out[...] = held[chip ^ k].astype(out.dtype)


def pack(a, b, c, d, gram_ref, out_ref):
    half, width = a.shape
    rank = 2 * half
    total = (a[...] + b[...].astype(f32)) + (c[...].astype(f32) + d[...].astype(f32))
    out_ref[:, :width] = total.astype(bf16)
    left = jnp.concatenate((gram_ref[:half, :], gram_ref[half:, :]), axis=1)
    for k in range(3):
        term = left.astype(bf16)
        left = left - term.astype(f32)
        out_ref[:, width + k * 128 : width + k * 128 + 2 * rank] = term


def unpack(a, b, c, d, out_ref, gram_ref):
    half, width = out_ref.shape
    rank = 2 * half

    def part(ref, at, count):
        return ref[:, at : at + count].astype(f32)

    out_ref[...] = (part(a, 0, width) + part(b, 0, width)) + (part(c, 0, width) + part(d, 0, width))
    grams = [sum(part(ref, width + k * 128, 2 * rank) for k in range(3)) for ref in (a, b, c, d)]
    total = (grams[0] + grams[1]) + (grams[2] + grams[3])
    gram_ref[:half, :] = total[:, :rank]
    gram_ref[half:, :] = total[:, rank:]


def invert_cholesky(g_ref, out_ref):
    n = g_ref.shape[0]
    rows = lax.broadcasted_iota(jnp.int32, (n, n), 0)
    cols = lax.broadcasted_iota(jnp.int32, (n, n), 1)
    a = g_ref[...]
    inverse = jnp.where(rows == cols, 1.0, 0.0).astype(f32)
    for j in range(0, n, 2):
        first = jnp.sum(jnp.where(cols == j, a, 0.0), axis=1, keepdims=True)
        second = jnp.sum(jnp.where(cols == j + 1, a, 0.0), axis=1, keepdims=True)
        row, row_inverse = a[j : j + 1, :], inverse[j : j + 1, :]
        factor = jnp.where(rows[:, :1] > j, first / first[j : j + 1, :], 0.0)
        step = factor[j + 1 : j + 2, :]
        next_row = a[j + 1 : j + 2, :] - step * row
        next_inverse = inverse[j + 1 : j + 2, :] - step * row_inverse
        second = second - factor * first[j + 1 : j + 2, :]
        next_factor = jnp.where(rows[:, :1] > j + 1, second / second[j + 1 : j + 2, :], 0.0)
        a = a - factor * row - next_factor * next_row
        inverse = inverse - factor * row_inverse - next_factor * next_inverse
    diagonal = jnp.sum(jnp.where(rows == cols, a, 0.0), axis=1, keepdims=True)
    out_ref[...] = inverse * lax.rsqrt(diagonal)


def arrange(place, dy_ref, main_ref, rest_ref, held):
    t = place[0]
    step = first_partner(t)
    tokens = rest_ref.shape[1]
    for k, source in enumerate((t, t ^ step, t ^ 3 ^ step, t ^ 3)):
        held[k * tokens : (k + 1) * tokens, :] = dy_ref[pl.ds(pl.multiple_of(source * tokens, tokens), tokens), :]
    main = main_ref.shape[1]
    main_ref[...] = held[:main, :].T
    rest_ref[...] = held[main:, :].T


def accumulate(first, lane, spans, main_ref, base_ref, *rest):
    sources, (acc_ref, x_ref, sems) = rest[: len(spans)], rest[len(spans) :]
    width = acc_ref.shape[1]
    copies, at = [], 0
    for k, (source, (begin, end)) in enumerate(zip(sources, spans)):
        part = source.at[pl.ds(begin, end - begin), pl.ds(first, width)]
        copies.append(pltpu.make_async_copy(part, x_ref.at[pl.ds(at, end - begin), :], sems.at[k]))
        at += end - begin
    for copy in copies:
        copy.start()
    for copy in copies:
        copy.wait()
    step, block = 256, acc_ref.shape[0] // 4
    for c in range(0, width, step):
        cols = slice(c, c + step)
        for r in range(0, acc_ref.shape[0], block):
            here = slice(r, r + block)
            term = dot(main_ref[here, lane : lane + at], x_ref[:, cols])
            acc_ref[here, cols] = term + base_ref[here, cols].astype(f32)


def finish(replicas, place, linv, p_ref, rest_ref, a0, a1, a2, a3, b0, b1, b2, b3, new_ref, left_ref, right_ref, held, nf4):
    t, core, chip = place[0], place[1], place[2]
    for k, (a, b) in enumerate(((a0, b0), (a1, b1), (a2, b2), (a3, b3))):
        held[chip ^ k, core] = a[...]
        held[chip ^ k, 1 - core] = b[...]
    parts, _, half, width = held.shape
    rank = 2 * half
    l_high, l_low = split(linv[...])
    both = jnp.concatenate((l_high, l_low), axis=0)
    for s in range(parts):
        t_high, t_low = split(held[s].reshape(rank, width))
        term = dot(both, t_high)
        nf = (term[:rank] + (term[rank:] + dot(l_high, t_low))) * (1.0 / replicas)
        nf4[s] = nf
        high, low = split(nf)
        at = slice(s * width, (s + 1) * width)
        right_ref[:rank, at] = high
        right_ref[rank : 2 * rank, at] = high
        right_ref[2 * rank :, at] = low
    new_ref[...] = nf4[t]
    term = dot(both, p_ref[...])
    high, low = split(-(term[:rank] + term[rank:]))
    base = rest_ref.shape[1]
    left_ref[:, :base] = rest_ref[...]
    left_ref[:, base:] = jnp.concatenate((high, low, high), axis=0).T


def rebuild(left_ref, right_ref, acc_0, acc_1, x_any, out_any, buffer, staged, sem, out_sems):
    rows = x_any.shape[0]
    fetch = pltpu.make_async_copy(x_any, buffer.at[pl.ds(0, rows), :], sem)
    fetch.start()
    buffer[rows:, :] = right_ref[...]
    fetch.wait()
    slots, hidden, width = staged.shape
    count = acc_0.shape[1] // width

    def put(i):
        columns = out_any.at[:, pl.ds(i * width, width)]
        return pltpu.make_async_copy(staged.at[i % slots], columns, out_sems.at[i % slots])

    block = hidden // 4
    for i in range(2 * count):
        if i >= slots:
            put(i - slots).wait()
        acc_ref, first = (acc_0, acc_1)[i // count], i % count * width
        for r in range(0, hidden, block):
            at = slice(r, r + block)
            total = acc_ref[at, first : first + width] + dot(left_ref[at, :], buffer[:, i * width : (i + 1) * width])
            staged[i % slots, at, :] = total.astype(bf16)
        put(i).start()
    for i in range(2 * count - slots, 2 * count):
        put(i).wait()


def after(value, *others):
    return lax.optimization_barrier((value, *others))[0]


def partners(value, axis, size, by):
    return [lax.ppermute(value, axis, [(i, i ^ k) for i in range(size)]) for k in by]


def body(activations, out_grad, error_state, right_factor):
    errors = error_state[0]
    n_dp, n_t = lax.axis_size("dp"), lax.axis_size("tensor")
    rows, rank = right_factor.shape
    tokens, features = activations.shape
    all_tokens, hidden = out_grad.shape
    half = rank // 2
    t, d = lax.axis_index("tensor"), lax.axis_index("dp")
    place = jnp.stack([t, d & 1, d >> 1]).astype(jnp.int32)
    along_t = functools.partial(partners, axis="tensor", size=n_t, by=(1, 2, 3))
    along_xy = functools.partial(partners, axis="dp", size=n_dp, by=(2, 4, 6))

    anywhere = pl.BlockSpec(memory_space=pl.ANY)
    vmem_spec = pl.BlockSpec(memory_space=pltpu.VMEM)
    smem_spec = pl.BlockSpec(memory_space=pltpu.SMEM)
    hbm_spec = pl.BlockSpec(memory_space=pltpu.HBM)

    def move(value, perm, *when):
        return lax.ppermute(after(value, *when), "tensor", perm)

    q_own = right_factor.T.astype(bf16)
    q_parts = along_t(q_own)

    main = 3 * tokens
    main_t, rest_t = call(
        arrange,
        [like((hidden, main), bf16), like((hidden, all_tokens - main), bf16)],
        place, out_grad,
        scratch=[pltpu.VMEM((all_tokens, hidden), bf16)],
    )
    (e_0,) = call(
        load_half,
        [like((hidden, features // 2), bf16)],
        errors,
        in_specs=[hbm_spec],
        scratch=[pltpu.SemaphoreType.DMA(())],
        vmem=46,
    )
    q_parts, _, e_0 = lax.optimization_barrier((q_parts, main_t, e_0))
    way_1, way_2 = [(0, 2), (2, 3), (3, 1), (1, 0)], [(0, 1), (1, 3), (3, 2), (2, 0)]
    q_full, y_own = call(
        project,
        [like((n_t, rank, rows), bf16), like((rank, tokens), f32)],
        place, q_own, *q_parts, activations,
    )
    y_parts = along_t(y_own)
    eq, e_1 = call(
        error_left,
        [like((rank, hidden), f32), like((hidden, features // 2), bf16)],
        q_full, e_0, errors,
        in_specs=[vmem_spec, vmem_spec, hbm_spec],
        scratch=[pltpu.SemaphoreType.DMA((n_t // 2,))],
        vmem=40,
    )
    held_errors = (e_0, e_1)
    y_parts[0] = after(y_parts[0], eq)
    x_first = move(activations, way_1, *y_parts)
    (p_local,) = call(
        left_factor,
        [like((rank, hidden), bf16)],
        place, eq, y_own, *y_parts, out_grad,
        scratch=[pltpu.VMEM((n_t, rank, tokens), f32)],
    )
    (p_other,) = partners(p_local, "dp", n_dp, (1,))
    p_chip = (p_local.astype(f32) + p_other.astype(f32)).astype(bf16)
    p_parts = along_xy(p_chip)
    p_total, gram, near_w, far_w = call(
        weigh,
        [like((rank, hidden), bf16), like((rank, rank), f32), like((2, rank, tokens), f32), like((2, rank, tokens), bf16)],
        place, p_chip, *p_parts, out_grad,
        scratch=[pltpu.VMEM((n_t, rank, tokens), f32)],
    )
    (got_w,) = partners(far_w, "tensor", n_t, (3,))
    (te,) = call(error_right, [like((rank, features), f32)], p_total, *held_errors)
    got_w = after(got_w, te)
    keep, given = call(
        right_term,
        [like((half, features), f32), like((half, features), f32)],
        place, near_w, got_w, te, activations, x_first,
        scratch=[pltpu.VMEM((2, half, features), f32)],
    )
    x_second = move(activations, way_2, p_total)
    got_w = after(got_w, te)
    keep, given = call(
        right_term,
        [like((half, features), f32), like((half, features), f32)],
        place, near_w, got_w, te, activations, x_first,
        scratch=[pltpu.VMEM((2, half, features), f32)],
    )
    (got,) = partners(given, "dp", n_dp, (1,))
    parts = call(
        cut,
        [like((half, rows), f32)] + [like((half, rows), bf16)] * 3,
        place, keep, got,
        flops=CUT_COST,
        scratch=[pltpu.VMEM((n_t, half, rows), f32)],
    )
    arrived = [
        lax.ppermute(m, "dp", [(i, i ^ (2 * k)) for i in range(n_dp)])
        for k, m in enumerate(parts)
        if k
    ]
    def add_tokens(k, cost, lane, base, spans, *sources):
        count = sum(end - begin for begin, end in spans)
        return call(
            functools.partial(accumulate, k * (features // 2), lane, spans),
            [like((hidden, features // 2), f32)],
            main_t, base, *sources,
            flops=cost,
            in_specs=[vmem_spec, vmem_spec] + [anywhere] * len(sources),
            scratch=[pltpu.VMEM((count, features // 2), bf16), pltpu.SemaphoreType.DMA((len(spans),))],
        )[0]

    early = 256 - tokens
    accs = [
        add_tokens(k, 0, 0, e_held, ((0, tokens), (0, early)), activations, x_first)
        for k, e_held in enumerate(held_errors)
    ]
    (mine,) = call(pack, [like((half, rows + 384), bf16)], parts[0], *arrived, gram)
    mine = after(mine, *accs)
    z1, z2, z3 = along_t(mine)
    x_third = move(x_first, way_1, z1, z2, z3)
    accs = [
        add_tokens(k, ACC_COST, 256, acc, ((early, tokens), (0, tokens)), x_first, x_second)
        for k, acc in enumerate(accs)
    ]
    mine, gram = call(unpack, [like((half, rows), f32), like((rank, rank), f32)], mine, z1, z2, z3)
    (linv,) = call(invert_cholesky, [like((rank, rank), f32)], gram)
    near = [mine] + along_xy(mine)
    near[1] = after(near[1], linv)
    far = [partners(v, "dp", n_dp, (1,))[0] for v in near]
    new_factor, left, right = call(
        functools.partial(finish, n_dp),
        [like((rank, rows), f32), like((hidden, tokens + 3 * rank), bf16), like((3 * rank, features), bf16)],
        place, linv, p_total, rest_t, *near, *far,
        scratch=[pltpu.VMEM((4, 2, half, rows), f32), pltpu.VMEM((n_t, rank, rows), f32)],
    )
    (new_error,) = call(
        rebuild,
        [like((hidden, features), bf16)],
        left, right, *accs, x_third,
        in_specs=[vmem_spec] * 4 + [anywhere],
        out_specs=[anywhere],
        scratch=[
            pltpu.VMEM((tokens + 3 * rank, features), bf16),
            pltpu.VMEM((4, hidden, 256), bf16),
            pltpu.SemaphoreType.DMA(()),
            pltpu.SemaphoreType.DMA((4,)),
        ],
    )
    return (new_error[None], new_factor.T)


def solution(mesh):
    placed = (
        P(("dp", "tensor"), None),
        P("dp", "tensor"),
        P("dp", "tensor", None),
        P("tensor", None),
    )
    fits = mesh.shape["dp"] == 8 and mesh.shape["tensor"] == 4
    return jax.shard_map(
        body if fits else plain_body,
        mesh=mesh,
        in_specs=placed,
        out_specs=(P("dp", "tensor", None), P("tensor", None)),
        check_vma=False,
    )
```

```python
import functools
import jax
import jax.numpy as jnp
from jax import lax
from jax.experimental import pallas as pl
from jax.experimental.pallas import tpu as pltpu
from jax.sharding import PartitionSpec as P

contract_first = (((0,), (0,)), ((), ()))
contract_last = (((1,), (1,)), ((), ()))
column_block = 8
bf16, f32 = jnp.bfloat16, jnp.float32
MIB = 1 << 20
CUT_COST, ACC_COST = 1_600_000_000, 2_000_000_000


def plain_body(activations, out_grad, error_state, right_factor):
    highest = lax.Precision.HIGHEST
    errors = error_state[0]
    rows_here = right_factor.shape[0]
    factor_full = lax.all_gather(right_factor, "tensor", axis=0, tiled=True)
    grad = lax.dot_general(
        out_grad,
        lax.all_gather(activations, "tensor", axis=0, tiled=True),
        contract_first,
        preferred_element_type=f32,
    )
    corrected = grad + errors.astype(f32)
    p_local = jnp.dot(corrected, factor_full, precision=highest)
    p_total = lax.psum(p_local.astype(bf16), "dp").astype(f32)
    p_basis = jnp.zeros_like(p_total)
    for block_index in range(p_total.shape[1] // column_block):
        first = block_index * column_block
        columns = p_total[:, first : first + column_block]
        coeffs, block_gram = lax.psum(
            (
                jnp.dot(p_basis.T, columns, precision=highest),
                jnp.dot(columns.T, columns, precision=highest),
            ),
            "tensor",
        )
        remainder = columns - jnp.dot(p_basis, coeffs, precision=highest)
        residual_gram = block_gram - jnp.dot(coeffs.T, coeffs, precision=highest)
        lower_factor = jnp.linalg.cholesky(residual_gram)
        orthonormal = lax.linalg.triangular_solve(
            lower_factor, remainder, left_side=False, lower=True, transpose_a=True
        )
        p_basis = p_basis.at[:, first : first + column_block].set(orthonormal)
    replicas = lax.axis_size("dp")
    term = lax.dot_general(corrected, p_basis, contract_first, precision=highest)
    summed = lax.psum(term, ("dp", "tensor")) / replicas
    new_error = (corrected - jnp.dot(p_basis, summed.T, precision=highest)).astype(bf16)
    new_factor = lax.dynamic_slice_in_dim(
        summed, lax.axis_index("tensor") * rows_here, rows_here, 0
    )
    return (new_error[None], new_factor)


def dot(a, b, dims=None, precision=None):
    if dims is None:
        dims = (((1,), (0,)), ((), ()))
    return lax.dot_general(a, b, dims, precision=precision, preferred_element_type=f32)


def split(v):
    high = v.astype(bf16)
    return high, (v - high.astype(f32)).astype(bf16)


def call(kernel, outs, *args, scratch=(), in_specs=None, out_specs=None, vmem=8, flops=0):
    vmem_spec = pl.BlockSpec(memory_space=pltpu.VMEM)
    if in_specs is None:
        in_specs = [
            pl.BlockSpec(memory_space=pltpu.SMEM) if a.dtype == jnp.int32 else vmem_spec
            for a in args
        ]
    if out_specs is None:
        out_specs = [vmem_spec] * len(outs)
    size = sum(a.size * a.dtype.itemsize for a in args) + sum(
        o.size * o.dtype.itemsize for o in outs
    )
    result = pl.pallas_call(
        kernel,
        out_shape=list(outs),
        in_specs=in_specs,
        out_specs=out_specs,
        scratch_shapes=list(scratch),
        compiler_params=pltpu.CompilerParams(vmem_limit_bytes=vmem * MIB),
        cost_estimate=pl.CostEstimate(flops=flops, bytes_accessed=size, transcendentals=0),
        name=kernel.__name__ if hasattr(kernel, "__name__") else kernel.func.__name__,
    )(*args)
    return result


def like(shape, dtype):
    return jax.ShapeDtypeStruct(shape, dtype)


def project(place, own, n1, n2, n3, x_ref, q_ref, y_ref):
    t = place[0]
    for k, part in enumerate((own, n1, n2, n3)):
        q_ref[t ^ k] = part[...]
    parts, _, width = q_ref.shape
    total = dot(q_ref[0], x_ref[:, :width], contract_last)
    for k in range(1, parts):
        total += dot(q_ref[k], x_ref[:, k * width : (k + 1) * width], contract_last)
    y_ref[...] = total


def load_half(e_any, e_ref, sem):
    copy = pltpu.make_async_copy(e_any.at[:, pl.ds(0, e_ref.shape[1])], e_ref, sem)
    copy.start()
    copy.wait()


def error_left(q_ref, e_0, e_any, out_ref, e_1, sems):
    parts, _, width = q_ref.shape
    half = parts // 2

    def load(k):
        return pltpu.make_async_copy(
            e_any.at[:, pl.ds((half + k) * width, width)], e_1.at[:, pl.ds(k * width, width)], sems.at[k]
        )

    for k in range(half):
        load(k).start()
    total = dot(q_ref[0], e_0[:, :width], contract_last)
    for k in range(1, half):
        total += dot(q_ref[k], e_0[:, k * width : (k + 1) * width], contract_last)
    for k in range(half):
        load(k).wait()
        total += dot(q_ref[half + k], e_1[:, k * width : (k + 1) * width], contract_last)
    out_ref[...] = total


def left_factor(place, eq_ref, own, n1, n2, n3, dy_ref, out_ref, y4):
    t = place[0]
    for k, part in enumerate((own, n1, n2, n3)):
        y4[t ^ k] = part[...]
    parts, rank, tokens = y4.shape
    total = eq_ref[...]
    for s in range(parts):
        both = jnp.concatenate(split(y4[s]), axis=0)
        term = dot(both, dy_ref[s * tokens : (s + 1) * tokens, :])
        total += term[:rank] + term[rank:]
    out_ref[...] = total.astype(bf16)


def first_partner(t):
    return jnp.where((t == 1) | (t == 2), 2, 1)


def weigh(place, own, n1, n2, n3, dy_ref, p_ref, gram_ref, near_ref, far_ref, held):
    t = place[0]
    p = (own[...].astype(f32) + n1[...].astype(f32)) + (n2[...].astype(f32) + n3[...].astype(f32))
    p = p.astype(bf16)
    p_ref[...] = p
    parts, _, tokens = held.shape
    gram_ref[...] = dot(p, p, contract_last)
    for s in range(parts):
        held[s] = dot(p, dy_ref[s * tokens : (s + 1) * tokens, :], contract_last)
    step = first_partner(t)
    near_ref[0] = held[t]
    near_ref[1] = held[t ^ step]
    far_ref[0] = held[t ^ 3].astype(bf16)
    far_ref[1] = held[t ^ 3 ^ step].astype(bf16)


def error_right(p_ref, e_0, e_1, out_ref):
    width = e_0.shape[1]
    step = 640
    for k, e_ref in enumerate((e_0, e_1)):
        for c in range(0, width, step):
            out_ref[:, k * width + c : k * width + c + step] = dot(p_ref[...], e_ref[:, c : c + step])


def right_term(place, near_ref, got_ref, te_ref, x_own, x_first, keep_ref, send_ref, held):
    core = place[1]
    rank = te_ref.shape[0]
    total = te_ref[...]
    for k, x_ref in enumerate((x_own, x_first)):
        both = jnp.concatenate(split(near_ref[k] + got_ref[k].astype(f32)), axis=0)
        term = dot(both, x_ref[...])
        total += term[:rank] + term[rank:]
    held[0] = total[: rank // 2]
    held[1] = total[rank // 2 :]
    keep_ref[...] = held[core]
    send_ref[...] = held[1 - core]


def cut(place, keep, got, o0, o1, o2, o3, held):
    chip = place[2]
    total = keep[...] + got[...]
    width = held.shape[2]
    for s in range(held.shape[0]):
        held[s] = total[:, s * width : (s + 1) * width]
    for k, out in enumerate((o0, o1, o2, o3)):
        out[...] = held[chip ^ k].astype(out.dtype)


def pack(a, b, c, d, gram_ref, out_ref):
    half, width = a.shape
    rank = 2 * half
    total = (a[...] + b[...].astype(f32)) + (c[...].astype(f32) + d[...].astype(f32))
    out_ref[:, :width] = total.astype(bf16)
    left = jnp.concatenate((gram_ref[:half, :], gram_ref[half:, :]), axis=1)
    terms = []
    for _ in range(3):
        terms.append(left.astype(bf16).astype(f32))
        left = left - terms[-1]
    terms.append(jnp.zeros_like(left))
    out_ref[:, width:] = jnp.concatenate(terms, axis=1).astype(bf16)


def unpack(a, b, c, d, out_ref, gram_ref):
    half, width = out_ref.shape
    rank = 2 * half

    def part(ref, at, count):
        return ref[:, at : at + count].astype(f32)

    out_ref[...] = (part(a, 0, width) + part(b, 0, width)) + (part(c, 0, width) + part(d, 0, width))
    grams = []
    for ref in (a, b, c, d):
        terms = part(ref, width, 8 * rank)
        grams.append(terms[:, : 2 * rank] + (terms[:, 2 * rank : 4 * rank] + terms[:, 4 * rank : 6 * rank]))
    total = (grams[0] + grams[1]) + (grams[2] + grams[3])
    gram_ref[:half, :] = total[:, :rank]
    gram_ref[half:, :] = total[:, rank:]


def invert_cholesky(g_ref, out_ref):
    n = g_ref.shape[0]
    rows = lax.broadcasted_iota(jnp.int32, (n, n), 0)
    cols = lax.broadcasted_iota(jnp.int32, (n, n), 1)
    a = g_ref[...]
    inverse = jnp.where(rows == cols, 1.0, 0.0).astype(f32)
    for j in range(0, n, 2):
        first = jnp.sum(jnp.where(cols == j, a, 0.0), axis=1, keepdims=True)
        second = jnp.sum(jnp.where(cols == j + 1, a, 0.0), axis=1, keepdims=True)
        row, row_inverse = a[j : j + 1, :], inverse[j : j + 1, :]
        factor = jnp.where(rows[:, :1] > j, first / first[j : j + 1, :], 0.0)
        step = factor[j + 1 : j + 2, :]
        next_row = a[j + 1 : j + 2, :] - step * row
        next_inverse = inverse[j + 1 : j + 2, :] - step * row_inverse
        second = second - factor * first[j + 1 : j + 2, :]
        next_factor = jnp.where(rows[:, :1] > j + 1, second / second[j + 1 : j + 2, :], 0.0)
        a = a - factor * row - next_factor * next_row
        inverse = inverse - factor * row_inverse - next_factor * next_inverse
    diagonal = jnp.sum(jnp.where(rows == cols, a, 0.0), axis=1, keepdims=True)
    out_ref[...] = inverse * lax.rsqrt(diagonal)


def arrange(place, dy_ref, main_ref, rest_ref, held):
    t = place[0]
    step = first_partner(t)
    tokens = rest_ref.shape[1]
    for k, source in enumerate((t, t ^ step, t ^ 3 ^ step, t ^ 3)):
        held[k * tokens : (k + 1) * tokens, :] = dy_ref[pl.ds(pl.multiple_of(source * tokens, tokens), tokens), :]
    main = main_ref.shape[1]
    main_ref[...] = held[:main, :].T
    rest_ref[...] = held[main:, :].T


def accumulate(first, lane, spans, main_ref, base_ref, *rest):
    sources, (acc_ref, x_ref, sems) = rest[: len(spans)], rest[len(spans) :]
    width = acc_ref.shape[1]
    copies, at = [], 0
    for k, (source, (begin, end)) in enumerate(zip(sources, spans)):
        part = source.at[pl.ds(begin, end - begin), pl.ds(first, width)]
        copies.append(pltpu.make_async_copy(part, x_ref.at[pl.ds(at, end - begin), :], sems.at[k]))
        at += end - begin
    for copy in copies:
        copy.start()
    for copy in copies:
        copy.wait()
    step, block = 256, acc_ref.shape[0] // 4
    for c in range(0, width, step):
        cols = slice(c, c + step)
        for r in range(0, acc_ref.shape[0], block):
            here = slice(r, r + block)
            term = dot(main_ref[here, lane : lane + at], x_ref[:, cols])
            acc_ref[here, cols] = term + base_ref[here, cols].astype(f32)


def finish(replicas, place, linv, p_ref, rest_ref, a0, a1, a2, a3, b0, b1, b2, b3, new_ref, left_ref, right_ref, held, nf4):
    t, core, chip = place[0], place[1], place[2]
    for k, (a, b) in enumerate(((a0, b0), (a1, b1), (a2, b2), (a3, b3))):
        held[chip ^ k, core] = a[...]
        held[chip ^ k, 1 - core] = b[...]
    parts, _, half, width = held.shape
    rank = 2 * half
    l_high, l_low = split(linv[...])
    both = jnp.concatenate((l_high, l_low), axis=0)
    for s in range(parts):
        t_high, t_low = split(held[s].reshape(rank, width))
        term = dot(both, t_high)
        nf = (term[:rank] + (term[rank:] + dot(l_high, t_low))) * (1.0 / replicas)
        nf4[s] = nf
        high, low = split(nf)
        at = slice(s * width, (s + 1) * width)
        right_ref[:rank, at] = high
        right_ref[rank : 2 * rank, at] = high
        right_ref[2 * rank :, at] = low
    new_ref[...] = nf4[t]
    term = dot(both, p_ref[...])
    high, low = split(-(term[:rank] + term[rank:]))
    base = rest_ref.shape[1]
    left_ref[:, :base] = rest_ref[...]
    left_ref[:, base:] = jnp.concatenate((high, low, high), axis=0).T


def rebuild(left_ref, right_ref, acc_0, acc_1, x_any, out_any, buffer, staged, sem, out_sems):
    rows = x_any.shape[0]
    fetch = pltpu.make_async_copy(x_any, buffer.at[pl.ds(0, rows), :], sem)
    fetch.start()
    buffer[rows:, :] = right_ref[...]
    fetch.wait()
    slots, hidden, width = staged.shape
    count = acc_0.shape[1] // width

    def put(i):
        columns = out_any.at[:, pl.ds(i * width, width)]
        return pltpu.make_async_copy(staged.at[i % slots], columns, out_sems.at[i % slots])

    block = hidden // 4
    for i in range(2 * count):
        if i >= slots:
            put(i - slots).wait()
        acc_ref, first = (acc_0, acc_1)[i // count], i % count * width
        for r in range(0, hidden, block):
            at = slice(r, r + block)
            total = acc_ref[at, first : first + width] + dot(left_ref[at, :], buffer[:, i * width : (i + 1) * width])
            staged[i % slots, at, :] = total.astype(bf16)
        put(i).start()
    for i in range(2 * count - slots, 2 * count):
        put(i).wait()


def after(value, *others):
    return lax.optimization_barrier((value, *others))[0]


def partners(value, axis, size, by):
    return [lax.ppermute(value, axis, [(i, i ^ k) for i in range(size)]) for k in by]


def body(activations, out_grad, error_state, right_factor):
    errors = error_state[0]
    n_dp, n_t = lax.axis_size("dp"), lax.axis_size("tensor")
    rows, rank = right_factor.shape
    tokens, features = activations.shape
    all_tokens, hidden = out_grad.shape
    half = rank // 2
    t, d = lax.axis_index("tensor"), lax.axis_index("dp")
    place = jnp.stack([t, d & 1, d >> 1]).astype(jnp.int32)
    along_t = functools.partial(partners, axis="tensor", size=n_t, by=(1, 2, 3))
    along_xy = functools.partial(partners, axis="dp", size=n_dp, by=(2, 4, 6))

    anywhere = pl.BlockSpec(memory_space=pl.ANY)
    vmem_spec = pl.BlockSpec(memory_space=pltpu.VMEM)
    smem_spec = pl.BlockSpec(memory_space=pltpu.SMEM)
    hbm_spec = pl.BlockSpec(memory_space=pltpu.HBM)

    def move(value, perm, *when):
        return lax.ppermute(after(value, *when), "tensor", perm)

    q_own = right_factor.T.astype(bf16)
    q_parts = along_t(q_own)

    main = 3 * tokens
    main_t, rest_t = call(
        arrange,
        [like((hidden, main), bf16), like((hidden, all_tokens - main), bf16)],
        place, out_grad,
        scratch=[pltpu.VMEM((all_tokens, hidden), bf16)],
    )
    (e_0,) = call(
        load_half,
        [like((hidden, features // 2), bf16)],
        errors,
        in_specs=[hbm_spec],
        scratch=[pltpu.SemaphoreType.DMA(())],
        vmem=46,
    )
    q_parts, _, e_0 = lax.optimization_barrier((q_parts, main_t, e_0))
    way_1, way_2 = [(0, 2), (2, 3), (3, 1), (1, 0)], [(0, 1), (1, 3), (3, 2), (2, 0)]
    q_full, y_own = call(
        project,
        [like((n_t, rank, rows), bf16), like((rank, tokens), f32)],
        place, q_own, *q_parts, activations,
    )
    y_parts = along_t(y_own)
    eq, e_1 = call(
        error_left,
        [like((rank, hidden), f32), like((hidden, features // 2), bf16)],
        q_full, e_0, errors,
        in_specs=[vmem_spec, vmem_spec, hbm_spec],
        scratch=[pltpu.SemaphoreType.DMA((n_t // 2,))],
        vmem=40,
    )
    held_errors = (e_0, e_1)
    y_parts[0] = after(y_parts[0], eq)
    x_first = move(activations, way_1, *y_parts)
    (p_local,) = call(
        left_factor,
        [like((rank, hidden), bf16)],
        place, eq, y_own, *y_parts, out_grad,
        scratch=[pltpu.VMEM((n_t, rank, tokens), f32)],
    )
    (p_other,) = partners(p_local, "dp", n_dp, (1,))
    p_chip = (p_local.astype(f32) + p_other.astype(f32)).astype(bf16)
    p_parts = along_xy(p_chip)
    p_total, gram, near_w, far_w = call(
        weigh,
        [like((rank, hidden), bf16), like((rank, rank), f32), like((2, rank, tokens), f32), like((2, rank, tokens), bf16)],
        place, p_chip, *p_parts, out_grad,
        scratch=[pltpu.VMEM((n_t, rank, tokens), f32)],
    )
    (got_w,) = partners(far_w, "tensor", n_t, (3,))
    (te,) = call(error_right, [like((rank, features), f32)], p_total, *held_errors)
    got_w = after(got_w, te)
    keep, given = call(
        right_term,
        [like((half, features), f32), like((half, features), f32)],
        place, near_w, got_w, te, activations, x_first,
        scratch=[pltpu.VMEM((2, half, features), f32)],
    )
    x_second = move(activations, way_2, p_total)
    got_w = after(got_w, te)
    keep, given = call(
        right_term,
        [like((half, features), f32), like((half, features), f32)],
        place, near_w, got_w, te, activations, x_first,
        scratch=[pltpu.VMEM((2, half, features), f32)],
    )
    (got,) = partners(given, "dp", n_dp, (1,))
    parts = call(
        cut,
        [like((half, rows), f32)] + [like((half, rows), bf16)] * 3,
        place, keep, got,
        flops=CUT_COST,
        scratch=[pltpu.VMEM((n_t, half, rows), f32)],
    )
    arrived = [
        lax.ppermute(m, "dp", [(i, i ^ (2 * k)) for i in range(n_dp)])
        for k, m in enumerate(parts)
        if k
    ]
    def add_tokens(k, cost, lane, base, spans, *sources):
        count = sum(end - begin for begin, end in spans)
        return call(
            functools.partial(accumulate, k * (features // 2), lane, spans),
            [like((hidden, features // 2), f32)],
            main_t, base, *sources,
            flops=cost,
            in_specs=[vmem_spec, vmem_spec] + [anywhere] * len(sources),
            scratch=[pltpu.VMEM((count, features // 2), bf16), pltpu.SemaphoreType.DMA((len(spans),))],
        )[0]

    early = 256 - tokens
    accs = [
        add_tokens(k, 0, 0, e_held, ((0, tokens), (0, early)), activations, x_first)
        for k, e_held in enumerate(held_errors)
    ]
    (mine,) = call(pack, [like((half, rows + 8 * rank), bf16)], parts[0], *arrived, gram)
    mine = after(mine, *accs)
    z1, z2, z3 = along_t(mine)
    x_third = move(x_first, way_1, z1, z2, z3)
    accs = [
        add_tokens(k, ACC_COST, 256, acc, ((early, tokens), (0, tokens)), x_first, x_second)
        for k, acc in enumerate(accs)
    ]
    mine, gram = call(unpack, [like((half, rows), f32), like((rank, rank), f32)], mine, z1, z2, z3)
    (linv,) = call(invert_cholesky, [like((rank, rank), f32)], gram)
    near = [mine] + along_xy(mine)
    near[1] = after(near[1], linv)
    far = [partners(v, "dp", n_dp, (1,))[0] for v in near]
    new_factor, left, right = call(
        functools.partial(finish, n_dp),
        [like((rank, rows), f32), like((hidden, tokens + 3 * rank), bf16), like((3 * rank, features), bf16)],
        place, linv, p_total, rest_t, *near, *far,
        scratch=[pltpu.VMEM((4, 2, half, rows), f32), pltpu.VMEM((n_t, rank, rows), f32)],
    )
    (new_error,) = call(
        rebuild,
        [like((hidden, features), bf16)],
        left, right, *accs, x_third,
        in_specs=[vmem_spec] * 4 + [anywhere],
        out_specs=[anywhere],
        scratch=[
            pltpu.VMEM((tokens + 3 * rank, features), bf16),
            pltpu.VMEM((5, hidden, 256), bf16),
            pltpu.SemaphoreType.DMA(()),
            pltpu.SemaphoreType.DMA((5,)),
        ],
    )
    return (new_error[None], new_factor.T)


def solution(mesh):
    placed = (
        P(("dp", "tensor"), None),
        P("dp", "tensor"),
        P("dp", "tensor", None),
        P("tensor", None),
    )
    fits = mesh.shape["dp"] == 8 and mesh.shape["tensor"] == 4
    return jax.shard_map(
        body if fits else plain_body,
        mesh=mesh,
        in_specs=placed,
        out_specs=(P("dp", "tensor", None), P("tensor", None)),
        check_vma=False,
    )
```

```python
import functools
import jax
import jax.numpy as jnp
from jax import lax
from jax.experimental import pallas as pl
from jax.experimental.pallas import tpu as pltpu
from jax.sharding import PartitionSpec as P

contract_first = (((0,), (0,)), ((), ()))
contract_last = (((1,), (1,)), ((), ()))
column_block = 8
bf16, f32 = jnp.bfloat16, jnp.float32
MIB = 1 << 20
CUT_COST, ACC_COST = 1_600_000_000, 2_000_000_000


def plain_body(activations, out_grad, error_state, right_factor):
    highest = lax.Precision.HIGHEST
    errors = error_state[0]
    rows_here = right_factor.shape[0]
    factor_full = lax.all_gather(right_factor, "tensor", axis=0, tiled=True)
    grad = lax.dot_general(
        out_grad,
        lax.all_gather(activations, "tensor", axis=0, tiled=True),
        contract_first,
        preferred_element_type=f32,
    )
    corrected = grad + errors.astype(f32)
    p_local = jnp.dot(corrected, factor_full, precision=highest)
    p_total = lax.psum(p_local.astype(bf16), "dp").astype(f32)
    p_basis = jnp.zeros_like(p_total)
    for block_index in range(p_total.shape[1] // column_block):
        first = block_index * column_block
        columns = p_total[:, first : first + column_block]
        coeffs, block_gram = lax.psum(
            (
                jnp.dot(p_basis.T, columns, precision=highest),
                jnp.dot(columns.T, columns, precision=highest),
            ),
            "tensor",
        )
        remainder = columns - jnp.dot(p_basis, coeffs, precision=highest)
        residual_gram = block_gram - jnp.dot(coeffs.T, coeffs, precision=highest)
        lower_factor = jnp.linalg.cholesky(residual_gram)
        orthonormal = lax.linalg.triangular_solve(
            lower_factor, remainder, left_side=False, lower=True, transpose_a=True
        )
        p_basis = p_basis.at[:, first : first + column_block].set(orthonormal)
    replicas = lax.axis_size("dp")
    term = lax.dot_general(corrected, p_basis, contract_first, precision=highest)
    summed = lax.psum(term, ("dp", "tensor")) / replicas
    new_error = (corrected - jnp.dot(p_basis, summed.T, precision=highest)).astype(bf16)
    new_factor = lax.dynamic_slice_in_dim(
        summed, lax.axis_index("tensor") * rows_here, rows_here, 0
    )
    return (new_error[None], new_factor)


def dot(a, b, dims=None, precision=None):
    if dims is None:
        dims = (((1,), (0,)), ((), ()))
    return lax.dot_general(a, b, dims, precision=precision, preferred_element_type=f32)


def split(v):
    high = v.astype(bf16)
    return high, (v - high.astype(f32)).astype(bf16)


def call(kernel, outs, *args, scratch=(), in_specs=None, out_specs=None, vmem=8, flops=0):
    vmem_spec = pl.BlockSpec(memory_space=pltpu.VMEM)
    if in_specs is None:
        in_specs = [
            pl.BlockSpec(memory_space=pltpu.SMEM) if a.dtype == jnp.int32 else vmem_spec
            for a in args
        ]
    if out_specs is None:
        out_specs = [vmem_spec] * len(outs)
    size = sum(a.size * a.dtype.itemsize for a in args) + sum(
        o.size * o.dtype.itemsize for o in outs
    )
    result = pl.pallas_call(
        kernel,
        out_shape=list(outs),
        in_specs=in_specs,
        out_specs=out_specs,
        scratch_shapes=list(scratch),
        compiler_params=pltpu.CompilerParams(vmem_limit_bytes=vmem * MIB),
        cost_estimate=pl.CostEstimate(flops=flops, bytes_accessed=size, transcendentals=0),
        name=kernel.__name__ if hasattr(kernel, "__name__") else kernel.func.__name__,
    )(*args)
    return result


def like(shape, dtype):
    return jax.ShapeDtypeStruct(shape, dtype)


def project(place, own, n1, n2, n3, x_ref, q_ref, y_ref):
    t = place[0]
    for k, part in enumerate((own, n1, n2, n3)):
        q_ref[t ^ k] = part[...]
    parts, _, width = q_ref.shape
    total = dot(q_ref[0], x_ref[:, :width], contract_last)
    for k in range(1, parts):
        total += dot(q_ref[k], x_ref[:, k * width : (k + 1) * width], contract_last)
    y_ref[...] = total.astype(bf16)


def load_half(e_any, e_ref, sem):
    copy = pltpu.make_async_copy(e_any.at[:, pl.ds(0, e_ref.shape[1])], e_ref, sem)
    copy.start()
    copy.wait()


def error_left(q_ref, e_0, e_any, out_ref, e_1, sems):
    parts, _, width = q_ref.shape
    half = parts // 2

    def load(k):
        return pltpu.make_async_copy(
            e_any.at[:, pl.ds((half + k) * width, width)], e_1.at[:, pl.ds(k * width, width)], sems.at[k]
        )

    for k in range(half):
        load(k).start()
    total = dot(q_ref[0], e_0[:, :width], contract_last)
    for k in range(1, half):
        total += dot(q_ref[k], e_0[:, k * width : (k + 1) * width], contract_last)
    for k in range(half):
        load(k).wait()
        total += dot(q_ref[half + k], e_1[:, k * width : (k + 1) * width], contract_last)
    out_ref[...] = total


def left_factor(place, eq_ref, own, n1, n2, n3, dy_ref, out_ref, y4):
    t = place[0]
    for k, part in enumerate((own, n1, n2, n3)):
        y4[t ^ k] = part[...]
    parts, rank, tokens = y4.shape
    total = eq_ref[...]
    for s in range(parts):
        total += dot(y4[s], dy_ref[s * tokens : (s + 1) * tokens, :])
    out_ref[...] = total.astype(bf16)


def first_partner(t):
    return jnp.where((t == 1) | (t == 2), 2, 1)


def weigh(place, own, n1, n2, n3, dy_ref, p_ref, gram_ref, near_ref, far_ref, held):
    t = place[0]
    p = (own[...].astype(f32) + n1[...].astype(f32)) + (n2[...].astype(f32) + n3[...].astype(f32))
    p = p.astype(bf16)
    p_ref[...] = p
    parts, _, tokens = held.shape
    gram_ref[...] = dot(p, p, contract_last)
    for s in range(parts):
        held[s] = dot(p, dy_ref[s * tokens : (s + 1) * tokens, :], contract_last)
    step = first_partner(t)
    near_ref[0] = held[t]
    near_ref[1] = held[t ^ step]
    far_ref[0] = held[t ^ 3].astype(bf16)
    far_ref[1] = held[t ^ 3 ^ step].astype(bf16)


def error_right(p_ref, e_0, e_1, out_ref):
    width = e_0.shape[1]
    step = 640
    for k, e_ref in enumerate((e_0, e_1)):
        for c in range(0, width, step):
            out_ref[:, k * width + c : k * width + c + step] = dot(p_ref[...], e_ref[:, c : c + step])


def right_term(place, near_ref, got_ref, te_ref, x_own, x_first, keep_ref, send_ref, held):
    core = place[1]
    rank = te_ref.shape[0]
    total = te_ref[...]
    for k, x_ref in enumerate((x_own, x_first)):
        both = jnp.concatenate(split(near_ref[k] + got_ref[k].astype(f32)), axis=0)
        term = dot(both, x_ref[...])
        total += term[:rank] + term[rank:]
    held[0] = total[: rank // 2]
    held[1] = total[rank // 2 :]
    keep_ref[...] = held[core]
    send_ref[...] = held[1 - core]


def cut(place, keep, got, o0, o1, o2, o3, held):
    chip = place[2]
    total = keep[...] + got[...]
    width = held.shape[2]
    for s in range(held.shape[0]):
        held[s] = total[:, s * width : (s + 1) * width]
    for k, out in enumerate((o0, o1, o2, o3)):
        out[...] = held[chip ^ k].astype(out.dtype)


def pack(a, b, c, d, gram_ref, out_ref):
    half, width = a.shape
    rank = 2 * half
    total = (a[...] + b[...].astype(f32)) + (c[...].astype(f32) + d[...].astype(f32))
    out_ref[:, :width] = total.astype(bf16)
    left = jnp.concatenate((gram_ref[:half, :], gram_ref[half:, :]), axis=1)
    terms = []
    for _ in range(3):
        terms.append(left.astype(bf16).astype(f32))
        left = left - terms[-1]
    terms.append(jnp.zeros_like(left))
    out_ref[:, width:] = jnp.concatenate(terms, axis=1).astype(bf16)


def unpack(a, b, c, d, out_ref, gram_ref):
    half, width = out_ref.shape
    rank = 2 * half

    def part(ref, at, count):
        return ref[:, at : at + count].astype(f32)

    out_ref[...] = (part(a, 0, width) + part(b, 0, width)) + (part(c, 0, width) + part(d, 0, width))
    grams = []
    for ref in (a, b, c, d):
        terms = part(ref, width, 8 * rank)
        grams.append(terms[:, : 2 * rank] + (terms[:, 2 * rank : 4 * rank] + terms[:, 4 * rank : 6 * rank]))
    total = (grams[0] + grams[1]) + (grams[2] + grams[3])
    gram_ref[:half, :] = total[:, :rank]
    gram_ref[half:, :] = total[:, rank:]


def invert_cholesky(g_ref, out_ref):
    n = g_ref.shape[0]
    rows = lax.broadcasted_iota(jnp.int32, (n, n), 0)
    cols = lax.broadcasted_iota(jnp.int32, (n, n), 1)
    a = g_ref[...]
    inverse = jnp.where(rows == cols, 1.0, 0.0).astype(f32)
    for j in range(0, n, 2):
        first = jnp.sum(jnp.where(cols == j, a, 0.0), axis=1, keepdims=True)
        second = jnp.sum(jnp.where(cols == j + 1, a, 0.0), axis=1, keepdims=True)
        row, row_inverse = a[j : j + 1, :], inverse[j : j + 1, :]
        factor = jnp.where(rows[:, :1] > j, first / first[j : j + 1, :], 0.0)
        step = factor[j + 1 : j + 2, :]
        next_row = a[j + 1 : j + 2, :] - step * row
        next_inverse = inverse[j + 1 : j + 2, :] - step * row_inverse
        second = second - factor * first[j + 1 : j + 2, :]
        next_factor = jnp.where(rows[:, :1] > j + 1, second / second[j + 1 : j + 2, :], 0.0)
        a = a - factor * row - next_factor * next_row
        inverse = inverse - factor * row_inverse - next_factor * next_inverse
    diagonal = jnp.sum(jnp.where(rows == cols, a, 0.0), axis=1, keepdims=True)
    out_ref[...] = inverse * lax.rsqrt(diagonal)


def arrange(place, dy_ref, main_ref, rest_ref, held):
    t = place[0]
    step = first_partner(t)
    tokens = rest_ref.shape[1]
    for k, source in enumerate((t, t ^ step, t ^ 3 ^ step, t ^ 3)):
        held[k * tokens : (k + 1) * tokens, :] = dy_ref[pl.ds(pl.multiple_of(source * tokens, tokens), tokens), :]
    main = main_ref.shape[1]
    main_ref[...] = held[:main, :].T
    rest_ref[...] = held[main:, :].T


def accumulate(first, lane, spans, main_ref, base_ref, *rest):
    sources, (acc_ref, x_ref, sems) = rest[: len(spans)], rest[len(spans) :]
    width = acc_ref.shape[1]
    copies, at = [], 0
    for k, (source, (begin, end)) in enumerate(zip(sources, spans)):
        part = source.at[pl.ds(begin, end - begin), pl.ds(first, width)]
        copies.append(pltpu.make_async_copy(part, x_ref.at[pl.ds(at, end - begin), :], sems.at[k]))
        at += end - begin
    for copy in copies:
        copy.start()
    for copy in copies:
        copy.wait()
    step, block = 256, acc_ref.shape[0] // 4
    for c in range(0, width, step):
        cols = slice(c, c + step)
        for r in range(0, acc_ref.shape[0], block):
            here = slice(r, r + block)
            term = dot(main_ref[here, lane : lane + at], x_ref[:, cols])
            acc_ref[here, cols] = term + base_ref[here, cols].astype(f32)


def finish(replicas, place, linv, p_ref, rest_ref, a0, a1, a2, a3, b0, b1, b2, b3, new_ref, left_ref, right_ref, held, nf4):
    t, core, chip = place[0], place[1], place[2]
    for k, (a, b) in enumerate(((a0, b0), (a1, b1), (a2, b2), (a3, b3))):
        held[chip ^ k, core] = a[...]
        held[chip ^ k, 1 - core] = b[...]
    parts, _, half, width = held.shape
    rank = 2 * half
    l_high, l_low = split(linv[...])
    both = jnp.concatenate((l_high, l_low), axis=0)
    for s in range(parts):
        t_high, t_low = split(held[s].reshape(rank, width))
        term = dot(both, t_high)
        nf = (term[:rank] + (term[rank:] + dot(l_high, t_low))) * (1.0 / replicas)
        nf4[s] = nf
        high, low = split(nf)
        at = slice(s * width, (s + 1) * width)
        right_ref[:rank, at] = high
        right_ref[rank : 2 * rank, at] = high
        right_ref[2 * rank :, at] = low
    new_ref[...] = nf4[t]
    term = dot(both, p_ref[...])
    high, low = split(-(term[:rank] + term[rank:]))
    base = rest_ref.shape[1]
    left_ref[:, :base] = rest_ref[...]
    left_ref[:, base:] = jnp.concatenate((high, low, high), axis=0).T


def rebuild(left_ref, right_ref, acc_0, acc_1, x_any, out_any, buffer, staged, sem, out_sems):
    rows = x_any.shape[0]
    fetch = pltpu.make_async_copy(x_any, buffer.at[pl.ds(0, rows), :], sem)
    fetch.start()
    buffer[rows:, :] = right_ref[...]
    fetch.wait()
    slots, hidden, width = staged.shape
    count = acc_0.shape[1] // width

    def put(i):
        columns = out_any.at[:, pl.ds(i * width, width)]
        return pltpu.make_async_copy(staged.at[i % slots], columns, out_sems.at[i % slots])

    block = hidden // 4
    for i in range(2 * count):
        if i >= slots:
            put(i - slots).wait()
        acc_ref, first = (acc_0, acc_1)[i // count], i % count * width
        for r in range(0, hidden, block):
            at = slice(r, r + block)
            total = acc_ref[at, first : first + width] + dot(left_ref[at, :], buffer[:, i * width : (i + 1) * width])
            staged[i % slots, at, :] = total.astype(bf16)
        put(i).start()
    for i in range(2 * count - slots, 2 * count):
        put(i).wait()


def after(value, *others):
    return lax.optimization_barrier((value, *others))[0]


def partners(value, axis, size, by):
    return [lax.ppermute(value, axis, [(i, i ^ k) for i in range(size)]) for k in by]


def body(activations, out_grad, error_state, right_factor):
    errors = error_state[0]
    n_dp, n_t = lax.axis_size("dp"), lax.axis_size("tensor")
    rows, rank = right_factor.shape
    tokens, features = activations.shape
    all_tokens, hidden = out_grad.shape
    half = rank // 2
    t, d = lax.axis_index("tensor"), lax.axis_index("dp")
    place = jnp.stack([t, d & 1, d >> 1]).astype(jnp.int32)
    along_t = functools.partial(partners, axis="tensor", size=n_t, by=(1, 2, 3))
    along_xy = functools.partial(partners, axis="dp", size=n_dp, by=(2, 4, 6))

    anywhere = pl.BlockSpec(memory_space=pl.ANY)
    vmem_spec = pl.BlockSpec(memory_space=pltpu.VMEM)
    smem_spec = pl.BlockSpec(memory_space=pltpu.SMEM)
    hbm_spec = pl.BlockSpec(memory_space=pltpu.HBM)

    def move(value, perm, *when):
        return lax.ppermute(after(value, *when), "tensor", perm)

    q_own = right_factor.T.astype(bf16)
    q_parts = along_t(q_own)

    main = 3 * tokens
    main_t, rest_t = call(
        arrange,
        [like((hidden, main), bf16), like((hidden, all_tokens - main), bf16)],
        place, out_grad,
        scratch=[pltpu.VMEM((all_tokens, hidden), bf16)],
    )
    (e_0,) = call(
        load_half,
        [like((hidden, features // 2), bf16)],
        errors,
        in_specs=[hbm_spec],
        scratch=[pltpu.SemaphoreType.DMA(())],
        vmem=46,
    )
    q_parts, _, e_0 = lax.optimization_barrier((q_parts, main_t, e_0))
    way_1, way_2 = [(0, 2), (2, 3), (3, 1), (1, 0)], [(0, 1), (1, 3), (3, 2), (2, 0)]
    q_full, y_own = call(
        project,
        [like((n_t, rank, rows), bf16), like((rank, tokens), bf16)],
        place, q_own, *q_parts, activations,
    )
    y_parts = along_t(y_own)
    eq, e_1 = call(
        error_left,
        [like((rank, hidden), f32), like((hidden, features // 2), bf16)],
        q_full, e_0, errors,
        in_specs=[vmem_spec, vmem_spec, hbm_spec],
        scratch=[pltpu.SemaphoreType.DMA((n_t // 2,))],
        vmem=40,
    )
    held_errors = (e_0, e_1)
    y_parts[0] = after(y_parts[0], eq)
    x_first = move(activations, way_1, *y_parts)
    (p_local,) = call(
        left_factor,
        [like((rank, hidden), bf16)],
        place, eq, y_own, *y_parts, out_grad,
        scratch=[pltpu.VMEM((n_t, rank, tokens), bf16)],
    )
    (p_other,) = partners(p_local, "dp", n_dp, (1,))
    p_chip = (p_local.astype(f32) + p_other.astype(f32)).astype(bf16)
    p_parts = along_xy(p_chip)
    p_total, gram, near_w, far_w = call(
        weigh,
        [like((rank, hidden), bf16), like((rank, rank), f32), like((2, rank, tokens), f32), like((2, rank, tokens), bf16)],
        place, p_chip, *p_parts, out_grad,
        scratch=[pltpu.VMEM((n_t, rank, tokens), f32)],
    )
    (got_w,) = partners(far_w, "tensor", n_t, (3,))
    (te,) = call(error_right, [like((rank, features), f32)], p_total, *held_errors)
    got_w = after(got_w, te)
    keep, given = call(
        right_term,
        [like((half, features), f32), like((half, features), f32)],
        place, near_w, got_w, te, activations, x_first,
        scratch=[pltpu.VMEM((2, half, features), f32)],
    )
    x_second = move(activations, way_2, p_total)
    got_w = after(got_w, te)
    keep, given = call(
        right_term,
        [like((half, features), f32), like((half, features), f32)],
        place, near_w, got_w, te, activations, x_first,
        scratch=[pltpu.VMEM((2, half, features), f32)],
    )
    (got,) = partners(given, "dp", n_dp, (1,))
    parts = call(
        cut,
        [like((half, rows), f32)] + [like((half, rows), bf16)] * 3,
        place, keep, got,
        flops=CUT_COST,
        scratch=[pltpu.VMEM((n_t, half, rows), f32)],
    )
    arrived = [
        lax.ppermute(m, "dp", [(i, i ^ (2 * k)) for i in range(n_dp)])
        for k, m in enumerate(parts)
        if k
    ]
    def add_tokens(k, cost, lane, base, spans, *sources):
        count = sum(end - begin for begin, end in spans)
        return call(
            functools.partial(accumulate, k * (features // 2), lane, spans),
            [like((hidden, features // 2), f32)],
            main_t, base, *sources,
            flops=cost,
            in_specs=[vmem_spec, vmem_spec] + [anywhere] * len(sources),
            scratch=[pltpu.VMEM((count, features // 2), bf16), pltpu.SemaphoreType.DMA((len(spans),))],
        )[0]

    early = 256 - tokens
    accs = [
        add_tokens(k, 0, 0, e_held, ((0, tokens), (0, early)), activations, x_first)
        for k, e_held in enumerate(held_errors)
    ]
    (mine,) = call(pack, [like((half, rows + 8 * rank), bf16)], parts[0], *arrived, gram)
    mine = after(mine, *accs)
    z1, z2, z3 = along_t(mine)
    x_third = move(x_first, way_1, z1, z2, z3)
    accs = [
        add_tokens(k, ACC_COST, 256, acc, ((early, tokens), (0, tokens)), x_first, x_second)
        for k, acc in enumerate(accs)
    ]
    mine, gram = call(unpack, [like((half, rows), f32), like((rank, rank), f32)], mine, z1, z2, z3)
    (linv,) = call(invert_cholesky, [like((rank, rank), f32)], gram)
    near = [mine] + along_xy(mine)
    near[1] = after(near[1], linv)
    far = [partners(v, "dp", n_dp, (1,))[0] for v in near]
    new_factor, left, right = call(
        functools.partial(finish, n_dp),
        [like((rank, rows), f32), like((hidden, tokens + 3 * rank), bf16), like((3 * rank, features), bf16)],
        place, linv, p_total, rest_t, *near, *far,
        scratch=[pltpu.VMEM((4, 2, half, rows), f32), pltpu.VMEM((n_t, rank, rows), f32)],
    )
    (new_error,) = call(
        rebuild,
        [like((hidden, features), bf16)],
        left, right, *accs, x_third,
        in_specs=[vmem_spec] * 4 + [anywhere],
        out_specs=[anywhere],
        scratch=[
            pltpu.VMEM((tokens + 3 * rank, features), bf16),
            pltpu.VMEM((5, hidden, 256), bf16),
            pltpu.SemaphoreType.DMA(()),
            pltpu.SemaphoreType.DMA((5,)),
        ],
    )
    return (new_error[None], new_factor.T)


def solution(mesh):
    placed = (
        P(("dp", "tensor"), None),
        P("dp", "tensor"),
        P("dp", "tensor", None),
        P("tensor", None),
    )
    fits = mesh.shape["dp"] == 8 and mesh.shape["tensor"] == 4
    return jax.shard_map(
        body if fits else plain_body,
        mesh=mesh,
        in_specs=placed,
        out_specs=(P("dp", "tensor", None), P("tensor", None)),
        check_vma=False,
    )
```
